32 devices in a mesh: sub: 4 (over x, core), tile: 8 (over z, y).
Axes of the slice: x: 2, y: 2, z: 4, core: 2. Of those that a mesh axis runs over, the one named last changes fastest.
Arguments:
- modes: bfloat16 [128, 768, 512], P(('sub', 'tile')), may hold values from -0.21875 to 0.21875
- coupling: bfloat16 [128, 8, 768, 128], P(('sub', 'tile')), may hold values from -0.796875 to 0.796875
- inv_eig: float32 [128, 512], P(('sub', 'tile')), may hold values from 0.1 to 1
- sub_rows: int32 [128], P(('sub', 'tile')), may hold values from 192 to 768
- adjacency: int32 [128, 8], P(('sub', 'tile')), may hold values from 0 to 511, as said below
- base_mass: float32 [512, 128, 128], P(('sub', 'tile')), may hold values from -0.5 to 0.5
- iface_modes: bfloat16 [65536, 2048], P(('sub', 'tile')), may hold values from -0.08984375 to 0.08984375
Outputs:
- reduced_mass: float32 [2048, 2048], P('sub', 'tile')
The draws below stay inside these ranges and needn't reach their ends.
Inputs may be any that keep to these rules, and one draw needn't show every extreme that they name: `adjacency`: interface block b is owned by device b // 16 in the order of the joined axes sub+tile. The substructures of one device link only to blocks whose owners have the same tile index; at most 8 links of one device go to blocks of one owner device, and on every device some owner receives exactly 8.
All inputs are finite; a program needn't handle non-finite values.
Results may differ from the reference program's by a relative error of at most 0.004.
Values may be sent and summed in bfloat16 or wider, within the bound.
No kernel may reach another device: no remote copies, remote signals or barrier semaphores. Data moves between devices by JAX's collectives and lax.ppermute only.
A program may use at most 128 MiB of HBM per device.

```python
import math
import jax
import jax.numpy as jnp
from jax import lax

MODES = 512
IB = 128
KI = 2048
ROWS = 768
SUBS_DEV = 4
ADJ = 8
BLK_DEV = 16
CAP = 8
SUBS = 128
NB = 512
N_SUB = 4
N_TILE = 8


def draw_sub_rows(key, part):
    first, second, third = jax.random.split(jax.random.fold_in(key, 11), 3)
    sizes = jax.random.randint(first, (SUBS,), ROWS // 4, ROWS + 1)
    upper = jax.random.randint(second, (), 0, SUBS)
    lower = (upper + 1 + jax.random.randint(third, (), 0, SUBS - 1)) % SUBS
    sizes = sizes.at[upper].set(ROWS).at[lower].set(ROWS // 4)
    return sizes.astype(jnp.int32)


def draw_adjacency(key, part):
    devices = N_SUB * N_TILE
    links = SUBS_DEV * ADJ
    pool = N_SUB * CAP

    def one_device(dev_key, device):
        kheavy, kperm, kmix, klocal = jax.random.split(dev_key, 4)
        heavy = jax.random.randint(kheavy, (), 0, N_SUB)
        owners = jax.random.permutation(kperm, pool) // CAP
        priority = jnp.where(owners == heavy, 0, pool) + jnp.arange(pool)
        chosen = owners[jnp.argsort(priority)][:links]
        chosen = chosen[jax.random.permutation(kmix, links)]
        local = jax.random.randint(klocal, (links,), 0, BLK_DEV)
        ids = (chosen * N_TILE + device % N_TILE) * BLK_DEV + local
        return ids.reshape(SUBS_DEV, ADJ)
    keys = jax.random.split(jax.random.fold_in(key, 23), devices)
    table = jax.vmap(one_device)(keys, jnp.arange(devices))
    return table.reshape(SUBS, ADJ).astype(jnp.int32)


def strengthened(result, stream_key, source, target, parts, factor):
    owner, partner = [(jnp.arange(result.shape[axis_at]) // (result.shape[axis_at] // parts)).reshape([-1 if axis == axis_at else 1 for axis in range(result.ndim)]) for axis_at in (source, target)]
    chosen = jax.random.permutation(stream_key, parts)[partner]
    strong = (owner == chosen) | (owner == (partner + parts // 2) % parts)
    return jnp.where(strong, factor * result, result)


def block_levels(own_key, extent, cuts, smallest, top_value):
    loudness, own = 1.0, jax.random.fold_in(own_key, 6)
    for axis_at, blocks in cuts:
        steps = jnp.exp(jax.random.uniform(jax.random.fold_in(own, axis_at), (blocks,), jnp.float32, smallest / len(cuts), top_value / len(cuts)))
        loudness = loudness * jnp.repeat(steps, extent[axis_at] // blocks).reshape([-1 if axis == axis_at else 1 for axis in range(len(extent))])
    return loudness


def normal_values(rng, extent, deviation, most, pieces=(), kind=jnp.bfloat16):
    loudness = block_levels(rng, extent, pieces, -0.22, 0.18) if pieces else 1.0
    values = jax.random.normal(rng, extent, jnp.float32) * deviation * loudness
    return jnp.minimum(jnp.maximum(values, -most), most).astype(kind)


def bell_draw_with(own_key, dims, deviation, limit, cuts, heavy, kind=jnp.bfloat16):
    array = deviation * jax.random.normal(own_key, dims, jnp.float32)
    if cuts:
        array = array * block_levels(own_key, dims, cuts, -0.22, 0.18)
    return jnp.clip(strengthened(array, jax.random.fold_in(own_key, 3), *heavy), -limit, limit).astype(kind)


def setup_inputs(seed: int = 0) -> dict:
    arg_keys = jax.random.split(jax.random.key(seed), 8)
    return {
        "modes": normal_values(arg_keys[0], (SUBS, ROWS, MODES), ROWS ** -0.5, 0.21875, ((0, 32),)),
        "coupling": normal_values(arg_keys[1], (SUBS, ADJ, ROWS, IB), 0.13, 0.796875, ((0, 32),)),
        "inv_eig": jnp.clip(jnp.exp(math.log(1.0) - 2.3025851 * jax.random.uniform(arg_keys[2], (SUBS, MODES), jnp.float32) ** block_levels(arg_keys[2], (SUBS, MODES), ((0, 32),), -0.2, 0.2)), 0.1, 1.0),
        "sub_rows": draw_sub_rows(jax.random.fold_in(arg_keys[7], 71), 0),
        "adjacency": draw_adjacency(jax.random.fold_in(arg_keys[7], 71), 0),
        "base_mass": normal_values(arg_keys[5], (NB, IB, IB), IB ** -0.5, 0.5, ((0, 32),), jnp.float32),
        "iface_modes": bell_draw_with(arg_keys[6], (NB * IB, KI), 0.015, 0.08984375, ((0, 32),), (0, 1, 32, 2.75)),
    }


def reduce_one(item):
    masked_s, coupling_s, inv_s = item
    reduced = jnp.einsum("rm,arc->amc", masked_s.astype(jnp.float32), coupling_s.astype(jnp.float32))
    reduced_b = reduced.astype(jnp.bfloat16)
    weighted = (reduced * inv_s[None, :, None]).astype(jnp.bfloat16)
    contrib = jnp.einsum("amc,amd->acd", weighted.astype(jnp.float32), reduced_b.astype(jnp.float32))
    return contrib.astype(jnp.bfloat16)


def reference(modes, coupling, inv_eig, sub_rows, adjacency, base_mass, iface_modes):
    live = (jnp.arange(ROWS, dtype=jnp.int32)[None, :] < sub_rows[:, None]).astype(jnp.bfloat16)
    masked = modes * live[:, :, None]
    contrib = lax.map(reduce_one, (masked, coupling, inv_eig))
    flat_links = contrib.reshape(SUBS * ADJ, IB, IB).astype(jnp.float32)
    assembled = base_mass + jax.ops.segment_sum(flat_links, adjacency.reshape(-1), num_segments=NB)
    mass_rounded = assembled.astype(jnp.bfloat16)
    psi_blocks = iface_modes.reshape(NB, IB, KI)

    def accumulate(total, item):
        mass_b, psi_b = item
        image = jnp.dot(mass_b, psi_b, preferred_element_type=jnp.float32).astype(jnp.bfloat16)
        return total + jnp.dot(psi_b.T, image, preferred_element_type=jnp.float32), None

    reduced_mass, unused = lax.scan(accumulate, jnp.zeros((KI, KI), jnp.float32), (mass_rounded, psi_blocks))
    return reduced_mass
```

```python
import functools

import jax
import jax.numpy as jnp
from jax import lax
from jax.experimental import pallas as pl
from jax.experimental.pallas import tpu as pltpu
from jax.sharding import PartitionSpec as P

CAP = 8
CORES = 2
VMEM_LIMIT = 48 * 1024 * 1024


def params():
    return pltpu.CompilerParams(vmem_limit_bytes=VMEM_LIMIT)


def contrib_kernel(n_x, blk_dev, n_tile, me_ref, rows_ref, adj_ref, modes_ref, coup_ref, inv_ref, *rest):
    outs, count_ref = rest[:n_x], rest[n_x]
    s = pl.program_id(0)
    n_sub = n_x * CORES
    links, rows, block = coup_ref.shape[1:]

    @pl.when(s == 0)
    def _():
        for i in range(n_sub):
            count_ref[i] = 0

    live = lax.broadcasted_iota(jnp.int32, (rows, 1), 0) < rows_ref[s]
    modes = jnp.where(live, modes_ref[0], jnp.zeros((), modes_ref.dtype))
    inv = inv_ref[pl.ds(s, 1), :]
    my_x = me_ref[0] // CORES
    step = 2 if links % 2 == 0 else 1
    for a in range(0, links, step):
        pair = jnp.concatenate([coup_ref[0, a + i] for i in range(step)], axis=1)
        red = lax.dot_general(
            pair, modes, (((0,), (0,)), ((), ())), preferred_element_type=jnp.float32
        )
        weighted = (red * inv).astype(jnp.bfloat16)
        red_b = red.astype(jnp.bfloat16)
        for i in range(step):
            part = slice(i * block, (i + 1) * block)
            contrib = lax.dot_general(
                weighted[part], red_b[part], (((1,), (1,)), ((), ())),
                preferred_element_type=jnp.float32,
            ).astype(jnp.bfloat16)
            target = adj_ref[s, a + i] // (blk_dev * n_tile)
            slot = count_ref[target]
            count_ref[target] = slot + 1
            x_rel = (target // CORES) ^ my_x
            place = (target % CORES) * CAP + slot
            for xr in range(n_x):
                @pl.when(x_rel == xr)
                def _(xr=xr):
                    outs[xr][place] = contrib


def make_contrib(me, modes, coupling, inv_eig, sub_rows, adjacency, n_x, n_tile, blk_dev):
    subs, rows, width = modes.shape
    links, block = coupling.shape[1], coupling.shape[3]
    smem = pl.BlockSpec(memory_space=pltpu.SMEM)
    out = jax.ShapeDtypeStruct((CORES * CAP, block, block), jnp.bfloat16)
    return pl.pallas_call(
        functools.partial(contrib_kernel, n_x, blk_dev, n_tile),
        grid=(subs,),
        in_specs=[
            smem, smem, smem,
            pl.BlockSpec((1, rows, width), lambda s: (s, 0, 0)),
            pl.BlockSpec((1, links, rows, block), lambda s: (s, 0, 0, 0)),
            pl.BlockSpec(inv_eig.shape, lambda s: (0, 0)),
        ],
        out_specs=[pl.BlockSpec(out.shape, lambda s: (0, 0, 0))] * n_x,
        out_shape=[out] * n_x,
        scratch_shapes=[pltpu.SMEM((n_x * CORES,), jnp.int32)],
        compiler_params=params(),
        name="contrib",
    )(me, sub_rows, adjacency, modes, coupling, inv_eig)


def sums_kernel(n_x, blk_dev, n_tile, me_ref, base_ref, *rest):
    adj = rest[:n_x]
    arrived = rest[n_x:2 * n_x]
    total_ref, send_ref, count_ref = rest[2 * n_x:]
    my_x, my_core = me_ref[0] // CORES, me_ref[0] % CORES
    total_ref[0] = base_ref[...]
    total_ref[1] = jnp.zeros_like(base_ref)
    links = adj[0].shape[1]
    for xr in range(n_x):
        for i in range(CORES):
            count_ref[i] = 0

        def body(link, carry, xr=xr):
            ident = adj[xr][link // links, link % links]
            owner = ident // (blk_dev * n_tile)

            @pl.when(owner // CORES == my_x)
            def _():
                core = owner % CORES
                slot = count_ref[core]
                count_ref[core] = slot + 1
                rel, local = core ^ my_core, ident % blk_dev
                total_ref[rel, local] += arrived[xr][core * CAP + slot].astype(jnp.float32)
            return carry

        lax.fori_loop(0, adj[xr].shape[0] * links, body, 0)
    send_ref[...] = total_ref[...].astype(jnp.bfloat16)


def make_sums(me, base, adjs, arrived, n_x, n_tile):
    blk_dev, block = base.shape[:2]
    smem = pl.BlockSpec(memory_space=pltpu.SMEM)
    vmem = pl.BlockSpec(memory_space=pltpu.VMEM)
    shape = (CORES, blk_dev, block, block)
    return pl.pallas_call(
        functools.partial(sums_kernel, n_x, blk_dev, n_tile),
        in_specs=[smem, vmem] + [smem] * n_x + [vmem] * n_x,
        out_specs=[vmem, vmem],
        out_shape=[
            jax.ShapeDtypeStruct(shape, jnp.float32),
            jax.ShapeDtypeStruct(shape, jnp.bfloat16),
        ],
        scratch_shapes=[pltpu.SMEM((CORES,), jnp.int32)],
        compiler_params=params(),
        name="sums",
    )(me, base, *adjs, *arrived)


def turn_kernel(cols_ref, psi_ref, out_ref):
    out_ref[0] = psi_ref[...].T


def turn(cols, psi, width):
    groups = cols.shape[0]
    depth = psi.shape[0]
    piece = min(depth, 1024)
    return pl.pallas_call(
        turn_kernel,
        grid_spec=pltpu.PrefetchScalarGridSpec(
            num_scalar_prefetch=1,
            grid=(groups, depth // piece),
            in_specs=[pl.BlockSpec((piece, width), lambda g, k, cols: (k, cols[g]))],
            out_specs=pl.BlockSpec((1, width, piece), lambda g, k, cols: (g, 0, k)),
        ),
        out_shape=jax.ShapeDtypeStruct((groups, width, depth), psi.dtype),
        compiler_params=params(),
        cost_estimate=pl.CostEstimate(
            flops=0, bytes_accessed=4 * groups * width * depth, transcendentals=0
        ),
        name="turn",
    )(cols, psi)


def left_kernel(total_ref, got_ref, own_ref, other_ref, out_ref):
    block = total_ref.shape[2]
    zero = jnp.zeros((block, block), jnp.bfloat16)
    rows = own_ref.shape[0] * own_ref.shape[1]
    for rel, psi_t in enumerate((own_ref, other_ref)):
        mass = (total_ref[rel] + got_ref[1 - rel].astype(jnp.float32)).astype(jnp.bfloat16)
        pair = jnp.concatenate(
            [
                jnp.concatenate([mass[0], zero], axis=1),
                jnp.concatenate([zero, mass[1]], axis=1),
            ],
            axis=0,
        )
        out_ref[rel] = jnp.dot(
            psi_t[...].reshape(rows, 2 * block), pair, preferred_element_type=jnp.float32
        ).astype(jnp.bfloat16)


def make_left(total, got, own_t, other_t):
    _, blk_dev, block, _ = total.shape
    groups, width, depth = own_t.shape
    rows = groups * width
    mass = pl.BlockSpec((CORES, 2, block, block), lambda j: (0, j, 0, 0))
    side = pl.BlockSpec((groups, width, 2 * block), lambda j: (0, 0, j))
    return pl.pallas_call(
        left_kernel,
        grid=(blk_dev // 2,),
        in_specs=[mass, mass, side, side],
        out_specs=pl.BlockSpec((CORES, rows, 2 * block), lambda j: (0, 0, j)),
        out_shape=jax.ShapeDtypeStruct((CORES, rows, depth), jnp.bfloat16),
        compiler_params=params(),
        cost_estimate=pl.CostEstimate(
            flops=4 * CORES * rows * depth * block, bytes_accessed=8 * rows * depth,
            transcendentals=0,
        ),
        name="left",
    )(total, got, own_t, other_t)


def product_kernel(spans, cols_ref, left_ref, own_ref, other_ref, *outs):
    y = pl.program_id(0)
    for yy, (lo, hi) in enumerate(spans):
        @pl.when(y == yy)
        def _(yy=yy, lo=lo, hi=hi):
            res = jnp.dot(left_ref[0, lo:hi], own_ref[...], preferred_element_type=jnp.float32)
            res += jnp.dot(left_ref[1, lo:hi], other_ref[...], preferred_element_type=jnp.float32)
            outs[yy][...] = res.astype(outs[yy].dtype)


def product(cols, left, own, other, width, spans, dtype):
    _, rows, depth = left.shape
    side = pl.BlockSpec((depth, width), lambda y, cols: (0, cols[y]))
    return pl.pallas_call(
        functools.partial(product_kernel, spans),
        grid_spec=pltpu.PrefetchScalarGridSpec(
            num_scalar_prefetch=1,
            grid=(2,),
            in_specs=[pl.BlockSpec((CORES, rows, depth), lambda y, cols: (0, 0, 0)), side, side],
            out_specs=[
                pl.BlockSpec((hi - lo, width), lambda y, cols: (0, 0)) for lo, hi in spans
            ],
        ),
        out_shape=[jax.ShapeDtypeStruct((hi - lo, width), dtype) for lo, hi in spans],
        compiler_params=params(),
        cost_estimate=pl.CostEstimate(
            flops=sum(4 * CORES * (hi - lo) * width * depth // 2 for lo, hi in spans),
            bytes_accessed=4 * CORES * depth * width, transcendentals=0,
        ),
        name="product",
    )(cols, left, own, other)


def on_device(modes, coupling, inv_eig, sub_rows, adjacency, base_mass, iface_modes):
    n_sub = lax.axis_size("sub")
    n_tile = lax.axis_size("tile")
    n_x = n_sub // CORES
    n_z = n_tile // 2
    blk_dev, block = base_mass.shape[:2]
    width = iface_modes.shape[1]
    band, tile = width // n_sub, width // n_tile
    half = band // 2
    sub, at = lax.axis_index("sub"), lax.axis_index("tile")
    my_x, my_core = sub // CORES, sub % CORES
    me = sub.reshape(1)

    def swap_core(v):
        return lax.ppermute(v, "sub", [(i, i ^ 1) for i in range(n_sub)])

    def swap_x(v, d):
        return lax.ppermute(v, "sub", [(i, i ^ (d * CORES)) for i in range(n_sub)])

    def swap_tile(v, d):
        return lax.ppermute(v, "tile", [(i, i ^ d) for i in range(n_tile)])

    other = swap_core(iface_modes)
    adjs = [adjacency] + [swap_x(adjacency, d) for d in range(1, n_x)]
    sent = make_contrib(
        me, modes, coupling, inv_eig, sub_rows, adjacency, n_x, n_tile, blk_dev
    )
    arrived = [sent[0]] + [swap_x(sent[d], d) for d in range(1, n_x)]
    total, share = make_sums(me, base_mass, adjs, arrived, n_x, n_tile)
    got = swap_core(share)

    order = [(d, 0) for d in range(1, n_x)] + [(d, 1) for d in range(n_x)] + [(0, 0)]
    row_cols = jnp.stack([((my_x ^ d) * CORES + my_core) * 2 + p for d, p in order])
    row_cols = row_cols.astype(jnp.int32)
    own_t = turn(row_cols, iface_modes, half)
    other_t = turn(row_cols, other, half)
    left = make_left(total, got, own_t, other_t)

    first, both = (n_x - 1) * half, (2 * n_x - 1) * half
    rows = 2 * n_x * half
    final = None
    chunks = sorted(range(n_z), key=lambda z: (-min(z, 2), z))
    for z in chunks:
        cols = jnp.stack([at ^ (2 * z + y) for y in range(2)]).astype(jnp.int32)
        out0, out1 = product(
            cols, left, iface_modes, other, tile, [(0, first), (0, both)], jnp.bfloat16
        )
        go_x = jnp.concatenate([out0, out1[:first]], axis=1)
        got_x = [swap_x(go_x[(d - 1) * half:d * half], d) for d in range(1, n_x)]
        got_y = swap_tile(out1[first:], 1)
        keep0, keep1 = product(
            cols, left, iface_modes, other, tile, [(first, rows), (both, rows)], jnp.float32
        )
        sum_a = jnp.concatenate([keep0[n_x * half:], keep1], axis=1)
        for v in got_x:
            sum_a = sum_a + v.astype(jnp.float32)
        sum_b = keep0[:n_x * half] + got_y.astype(jnp.float32)
        next_y = swap_tile(sum_a[:, tile:].astype(jnp.bfloat16), 1)
        next_x = [
            swap_x(sum_b[d * half:(d + 1) * half].astype(jnp.bfloat16), d)
            for d in range(1, n_x)
        ]
        low = sum_a[:, :tile] + next_y.astype(jnp.float32)
        high = sum_b[:half]
        for v in next_x:
            high = high + v.astype(jnp.float32)
        mine = jnp.concatenate([low, high], axis=0)
        if z:
            mine = swap_tile(mine.astype(jnp.bfloat16), 2 * z).astype(jnp.float32)
        final = mine if final is None else final + mine
    return final


def solution(mesh):
    placed = (
        P(("sub", "tile"), None, None),
        P(("sub", "tile"), None, None, None),
        P(("sub", "tile"), None),
        P(("sub", "tile")),
        P(("sub", "tile"), None),
        P(("sub", "tile"), None, None),
        P(("sub", "tile"), None),
    )
    return jax.shard_map(
        on_device, mesh=mesh, in_specs=placed, out_specs=P("sub", "tile"), check_vma=False
    )
```

```python
import functools

import jax
import jax.numpy as jnp
from jax import lax
from jax.experimental import pallas as pl
from jax.experimental.pallas import tpu as pltpu
from jax.sharding import PartitionSpec as P

CAP = 8
CORES = 2
MIB = 1024 * 1024
SMEM = pl.BlockSpec(memory_space=pltpu.SMEM)
VMEM = pl.BlockSpec(memory_space=pltpu.VMEM)


def params(mib):
    return pltpu.CompilerParams(vmem_limit_bytes=mib * MIB)


def cheap():
    return pl.CostEstimate(flops=1, bytes_accessed=1, transcendentals=0)


ANY = pl.BlockSpec(memory_space=pl.ANY)


def contrib_kernel(
    owner_links, spot_ref, rows_ref, adj_ref, modes_ref, coup_ref, inv_ref, *refs
):
    outs, (part_ref, all_ref, count_ref) = refs[:-3], refs[-3:]
    s = pl.program_id(0)
    links, rows, block = coup_ref.shape[1:]

    @pl.when(s == 0)
    def _():
        for i in range(count_ref.shape[0]):
            count_ref[i] = 0

    live = lax.broadcasted_iota(jnp.int32, (rows, 1), 0) < rows_ref[s]
    modes = jnp.where(live, modes_ref[0], jnp.zeros((), modes_ref.dtype))
    inv = inv_ref[pl.ds(s, 1), :]
    wide = jnp.concatenate([coup_ref[0, a] for a in range(links)], axis=1)
    red = lax.dot_general(
        wide, modes, (((0,), (0,)), ((), ())), preferred_element_type=jnp.float32
    )
    weighted = (red * inv).astype(jnp.bfloat16)
    red_b = red.astype(jnp.bfloat16)
    for a in range(links):
        part = slice(a * block, (a + 1) * block)
        part_ref[a] = lax.dot_general(
            weighted[part], red_b[part], (((1,), (1,)), ((), ())),
            preferred_element_type=jnp.float32,
        ).astype(jnp.bfloat16)
    for a in range(links):
        target = adj_ref[s, a] // owner_links
        slot = count_ref[target]
        count_ref[target] = slot + 1
        all_ref[(target ^ spot_ref[0]) * CAP + slot] = part_ref[a]

    @pl.when(s == pl.num_programs(0) - 1)
    def _():
        for d, out in enumerate(outs):
            out[...] = all_ref[d * CAP:(d + 1) * CAP]


def make_contrib(spot, modes, coupling, inv_eig, sub_rows, adjacency, n_sub, owner_links):
    subs, rows, width = modes.shape
    links, block = coupling.shape[1], coupling.shape[3]
    out = jax.ShapeDtypeStruct((CAP, block, block), jnp.bfloat16)
    return pl.pallas_call(
        functools.partial(contrib_kernel, owner_links),
        grid=(subs,),
        in_specs=[
            SMEM, SMEM, SMEM,
            pl.BlockSpec((1, rows, width), lambda s: (s, 0, 0)),
            pl.BlockSpec((1, links, rows, block), lambda s: (s, 0, 0, 0)),
            pl.BlockSpec(inv_eig.shape, lambda s: (0, 0)),
        ],
        out_specs=[pl.BlockSpec(out.shape, lambda s: (0, 0, 0))] * n_sub,
        out_shape=[out] * n_sub,
        scratch_shapes=[
            pltpu.VMEM((links, block, block), jnp.bfloat16),
            pltpu.VMEM((n_sub * CAP, block, block), jnp.bfloat16),
            pltpu.SMEM((n_sub,), jnp.int32),
        ],
        compiler_params=params(60),
        cost_estimate=cheap(),
        name="contrib",
    )(spot, sub_rows, adjacency, modes, coupling, inv_eig)


def near_kernel(n_sub, base_ref, *rest):
    lists = rest[:n_sub]
    own_ref, pair_ref, total_ref, place_ref = rest[n_sub:]
    spare = base_ref.shape[0]
    total_ref[:spare] = base_ref[...]
    subs, links = lists[0].shape
    for i in range(n_sub * CAP):
        place_ref[i] = spare
    for d in range(n_sub):
        def body(link, slot, d=d):
            local = lists[d][link // links, link % links]

            @pl.when(local >= 0)
            def _():
                place_ref[d * CAP + slot] = local

            return slot + (local >= 0).astype(jnp.int32)

        lax.fori_loop(0, subs * links, body, jnp.int32(0))
    for d, group in enumerate((own_ref, pair_ref)):
        for i in range(CAP):
            total_ref[place_ref[d * CAP + i]] += group[i].astype(jnp.float32)


def make_near(base, lists, own, pair):
    blk_dev, block = base.shape[:2]
    n_sub = len(lists)
    return pl.pallas_call(
        functools.partial(near_kernel, n_sub),
        in_specs=[VMEM] + [SMEM] * n_sub + [VMEM] * 2,
        out_specs=[VMEM, SMEM],
        out_shape=[
            jax.ShapeDtypeStruct((blk_dev + 1, block, block), jnp.float32),
            jax.ShapeDtypeStruct((n_sub * CAP,), jnp.int32),
        ],
        compiler_params=params(12),
        cost_estimate=cheap(),
        name="near",
    )(base, *lists, own, pair)


def far_kernel(groups, place_ref, near_ref, *rest):
    mass_ref, total_ref = rest[-2:]
    total_ref[...] = near_ref[...]
    for d, group in enumerate(rest[:groups]):
        for i in range(CAP):
            total_ref[place_ref[(d + CORES) * CAP + i]] += group[i].astype(jnp.float32)
    mass_ref[...] = total_ref[:mass_ref.shape[0]].astype(jnp.bfloat16)


def make_far(place, near, groups, behind):
    count, block = near.shape[:2]
    return pl.pallas_call(
        functools.partial(far_kernel, len(groups)),
        in_specs=[SMEM, VMEM] + [VMEM] * len(groups) + [ANY] * len(behind),
        out_specs=VMEM,
        out_shape=jax.ShapeDtypeStruct((count - 1, block, block), jnp.bfloat16),
        scratch_shapes=[pltpu.VMEM(near.shape, jnp.float32)],
        compiler_params=params(12),
        cost_estimate=cheap(),
        name="far",
    )(place, near, *groups, *behind)


def turn_kernel(spot_ref, psi_ref, out_ref):
    groups, half, _ = out_ref.shape
    n_x = groups // 2
    x = pl.program_id(0)
    out_ref[jnp.where(x == 0, groups - 1, x - 1)] = psi_ref[:, :half].T
    out_ref[n_x - 1 + x] = psi_ref[:, half:].T


def turn(spot, psi, n_x, band):
    depth = psi.shape[0]
    shape = (2 * n_x, band // 2, depth)
    return pl.pallas_call(
        turn_kernel,
        grid_spec=pltpu.PrefetchScalarGridSpec(
            num_scalar_prefetch=1,
            grid=(n_x,),
            in_specs=[pl.BlockSpec((depth, band), lambda x, spot: (0, spot[0] ^ (x * CORES)))],
            out_specs=pl.BlockSpec(shape, lambda x, spot: (0, 0, 0)),
        ),
        out_shape=jax.ShapeDtypeStruct(shape, psi.dtype),
        compiler_params=params(16),
        cost_estimate=cheap(),
        name="turn",
    )(spot, psi)


def left_kernel(mass_ref, turned_ref, out_ref):
    block = mass_ref.shape[1]
    zero = jnp.zeros((block, block), jnp.bfloat16)
    groups, half, _ = turned_ref.shape
    for j in range(0, mass_ref.shape[0], 2):
        pair = jnp.concatenate(
            [
                jnp.concatenate([mass_ref[j], zero], axis=1),
                jnp.concatenate([zero, mass_ref[j + 1]], axis=1),
            ],
            axis=0,
        )
        cols = slice(j * block, (j + 2) * block)
        out_ref[:, cols] = jnp.dot(
            turned_ref[:, :, cols].reshape(groups * half, 2 * block), pair,
            preferred_element_type=jnp.float32,
        ).astype(jnp.bfloat16)


def make_left(mass, turned):
    groups, half, depth = turned.shape
    return pl.pallas_call(
        left_kernel,
        in_specs=[VMEM, VMEM],
        out_specs=VMEM,
        out_shape=jax.ShapeDtypeStruct((groups * half, depth), jnp.bfloat16),
        compiler_params=params(16),
        cost_estimate=cheap(),
        name="left",
    )(mass, turned)


def product_kernel(z, n_x, pairs, acc_in, go, keep, behind, spot_ref, *refs):
    lefts, psis, refs = refs[:pairs], refs[pairs:2 * pairs], refs[2 * pairs:]
    acc_x, acc_y = (refs[:n_x - 1], refs[n_x - 1]) if acc_in else (None, None)
    outs = refs[(n_x if acc_in else 0) + behind:]
    go_x, go_y = (outs[:n_x - 1], outs[n_x - 1]) if go else (None, None)
    keep_a, keep_b = outs[-2:] if keep else (None, None)
    rows = lefts[0].shape[0]
    half = rows // (2 * n_x)
    first, both = (n_x - 1) * half, (2 * n_x - 1) * half
    width = (go_y if go else keep_b).shape[1]
    for y in range(2):
        lo = 0 if go else (both if y else first)
        hi = rows if keep else (both if y else first)
        tile = spot_ref[1] ^ (2 * z + y)
        at = pl.ds(pl.multiple_of(tile * width, width), width)
        res = None
        for left, psi in zip(lefts, psis):
            term = jnp.dot(left[lo:hi], psi[:, at], preferred_element_type=jnp.float32)
            res = term if res is None else res + term
        here = slice(y * width, (y + 1) * width)
        if go:
            for d in range(n_x - 1):
                head = res[d * half:(d + 1) * half]
                if acc_in:
                    head += acc_x[d][:, here]
                go_x[d][:, here] = head.astype(go_x[d].dtype)
            if y:
                head = res[first:both]
                if acc_in:
                    head += acc_y[...]
                go_y[...] = head.astype(go_y.dtype)
        if keep:
            if not y:
                keep_b[...] = res[first - lo:both - lo]
            keep_a[:, here] = res[both - lo:]


def product(z, spot, lefts, psis, width, n_x, go=None, keep=False, accs=(), behind=()):
    rows = lefts[0].shape[0]
    half = rows // (2 * n_x)
    shapes = []
    if go is not None:
        shapes += [(half, 2 * width, go)] * (n_x - 1) + [(n_x * half, width, go)]
    if keep:
        shapes += [(half, 2 * width, jnp.float32), (n_x * half, width, jnp.float32)]
    return pl.pallas_call(
        functools.partial(
            product_kernel, z, n_x, len(lefts), bool(accs), go is not None, keep, len(behind)
        ),
        in_specs=[SMEM] + [VMEM] * (2 * len(lefts) + len(accs)) + [ANY] * len(behind),
        out_specs=[VMEM] * len(shapes),
        out_shape=[jax.ShapeDtypeStruct((r, c), t) for r, c, t in shapes],
        compiler_params=params(24),
        cost_estimate=cheap(),
        name="product",
    )(spot, *lefts, *psis, *accs, *behind)


def first_kernel(n_x, a_ref, b_ref, *refs):
    got_x, got_y, outs = refs[:n_x - 1], refs[n_x - 1], refs[n_x:]
    low, high, go_y, go_x = outs[0], outs[1], outs[2], outs[3:]
    half, width = low.shape
    total = a_ref[...]
    for v in got_x:
        total += v[...].astype(jnp.float32)
    low[...] = total[:, :width]
    go_y[...] = total[:, width:].astype(jnp.bfloat16)
    for d in range(n_x):
        rows = slice(d * half, (d + 1) * half)
        total = b_ref[rows] + got_y[rows].astype(jnp.float32)
        if d == 0:
            high[...] = total
        else:
            go_x[d - 1][...] = total.astype(jnp.bfloat16)


def add_first(keep_a, keep_b, got_x, got_y):
    half, width = keep_a.shape[0], keep_b.shape[1]
    n_x = len(got_x) + 1
    types = [jnp.float32] * 2 + [jnp.bfloat16] * n_x
    low, high, go_y, *go_x = pl.pallas_call(
        functools.partial(first_kernel, n_x),
        in_specs=[VMEM] * (n_x + 2),
        out_specs=[VMEM] * len(types),
        out_shape=[jax.ShapeDtypeStruct((half, width), t) for t in types],
        compiler_params=params(12),
        cost_estimate=cheap(),
        name="add_first",
    )(keep_a, keep_b, *got_x, got_y)
    return low, high, go_y, go_x


def second_kernel(n_x, low_ref, high_ref, got_y, *refs):
    got_x, tails, out = refs[:n_x - 1], refs[n_x - 1:-1], refs[-1]
    half = low_ref.shape[0]
    low = low_ref[...] + got_y[...].astype(jnp.float32)
    high = high_ref[...]
    for v in got_x:
        high += v[...].astype(jnp.float32)
    for v in tails:
        low += v[:half].astype(jnp.float32)
        high += v[half:].astype(jnp.float32)
    out[:half] = low.astype(out.dtype)
    out[half:] = high.astype(out.dtype)


def add_second(low, high, got_y, got_x, dtype, tails=()):
    half, width = low.shape
    return pl.pallas_call(
        functools.partial(second_kernel, len(got_x) + 1),
        in_specs=[VMEM] * (3 + len(got_x) + len(tails)),
        out_specs=VMEM,
        out_shape=jax.ShapeDtypeStruct((2 * half, width), dtype),
        compiler_params=params(12),
        cost_estimate=cheap(),
        name="add_second",
    )(low, high, got_y, *got_x, *tails)


def on_device(modes, coupling, inv_eig, sub_rows, adjacency, base_mass, iface_modes):
    n_sub = lax.axis_size("sub")
    n_tile = lax.axis_size("tile")
    n_x = n_sub // CORES
    n_z = n_tile // 2
    blk_dev = base_mass.shape[0]
    owner_links = blk_dev * n_tile
    width = iface_modes.shape[1]
    band, tile = width // n_sub, width // n_tile
    sub, at = lax.axis_index("sub"), lax.axis_index("tile")
    spot = jnp.stack([sub, at]).astype(jnp.int32)

    def swap_sub(v, d):
        return lax.ppermute(v, "sub", [(i, i ^ d) for i in range(n_sub)])

    def swap_x(v, d):
        return swap_sub(v, d * CORES)

    def swap_tile(v, d):
        return lax.ppermute(v, "tile", [(i, i ^ d) for i in range(n_tile)])

    owner, local = adjacency // owner_links, adjacency % blk_dev
    lists = [jnp.where(owner == (sub ^ d), local, -1) for d in range(n_sub)]
    lists = [swap_sub(v, d) if d else v for d, v in enumerate(lists)]
    other = swap_sub(iface_modes, 1)
    sent = make_contrib(
        spot, modes, coupling, inv_eig, sub_rows, adjacency, n_sub, owner_links
    )
    far = [swap_sub(sent[d], d) for d in range(CORES, n_sub)]
    near, place = make_near(base_mass, lists, sent[0], swap_sub(sent[1], 1))
    own_t = turn(spot, iface_modes, n_x, band)
    other_t = turn(spot, other, n_x, band)
    mass = make_far(place, near, far, [own_t, other_t])
    mass_other = swap_sub(mass, 1)
    left = make_left(mass, own_t)

    chunks = sorted(range(1, n_z), key=lambda z: (-min(z, 2), z)) + [0]
    head = product(chunks[0], spot, [left], [iface_modes], tile, n_x, go=jnp.float32)
    left_other = make_left(mass_other, other_t)
    lefts, psis = [left, left_other], [iface_modes, other]

    def send_first(go):
        *go_x, go_y = go
        return [swap_x(v, d + 1) for d, v in enumerate(go_x)], swap_tile(go_y, 1)

    def send_second(low, high, go_y, go_x):
        return low, high, swap_tile(go_y, 1), [swap_x(v, d + 1) for d, v in enumerate(go_x)]

    keep, first, second, third = {}, {}, {}, []
    last = len(chunks) - 1
    for i in range(last + 3):
        if i == 0:
            go = product(
                chunks[0], spot, [left_other], [other], tile, n_x, go=jnp.bfloat16, accs=head
            )
            first[0] = send_first(go)
            keep[0] = product(chunks[0], spot, lefts, psis, tile, n_x, keep=True, behind=go[:1])
        elif i <= last:
            behind = [keep[0][0]] if i == 1 else [second[i - 2][0]]
            *go, keep_a, keep_b = product(
                chunks[i], spot, lefts, psis, tile, n_x, go=jnp.bfloat16, keep=True,
                behind=behind,
            )
            keep[i] = keep_a, keep_b
            first[i] = send_first(go)
        if 0 < i <= last + 1:
            second[i - 1] = send_second(*add_first(*keep[i - 1], *first[i - 1]))
        if 1 < i < last + 2:
            mine = add_second(*second[i - 2], jnp.bfloat16)
            third.append(swap_tile(mine, 2 * chunks[i - 2]))
    return add_second(*second[last], jnp.float32, third)


def solution(mesh):
    placed = (
        P(("sub", "tile"), None, None),
        P(("sub", "tile"), None, None, None),
        P(("sub", "tile"), None),
        P(("sub", "tile")),
        P(("sub", "tile"), None),
        P(("sub", "tile"), None, None),
        P(("sub", "tile"), None),
    )
    return jax.shard_map(
        on_device, mesh=mesh, in_specs=placed, out_specs=P("sub", "tile"), check_vma=False
    )
```

```python
import functools

import jax
import jax.numpy as jnp
from jax import lax
from jax.experimental import pallas as pl
from jax.experimental.pallas import tpu as pltpu
from jax.sharding import PartitionSpec as P

CAP = 8
CORES = 2
MIB = 1024 * 1024
SMEM = pl.BlockSpec(memory_space=pltpu.SMEM)
VMEM = pl.BlockSpec(memory_space=pltpu.VMEM)


def params(mib):
    return pltpu.CompilerParams(vmem_limit_bytes=mib * MIB)


def cheap():
    return pl.CostEstimate(flops=1, bytes_accessed=1, transcendentals=0)


ANY = pl.BlockSpec(memory_space=pl.ANY)


def prep_kernel(owner_links, blk_dev, n_sub, adj_ref, spot_ref, dest_ref, *refs):
    lists, (flat_ref, count_ref) = refs[:n_sub], refs[n_sub:]
    sub = lax.axis_index("sub")
    spot_ref[0] = sub
    spot_ref[1] = lax.axis_index("tile")
    subs, links = adj_ref.shape
    for d in range(n_sub):
        count_ref[d] = 0
        for i in range(CAP):
            flat_ref[d * CAP + i] = blk_dev
    for s in range(subs):
        for a in range(links):
            ident = adj_ref[s, a]
            rel = (ident // owner_links) ^ sub
            slot = count_ref[rel]
            count_ref[rel] = slot + 1
            flat_ref[rel * CAP + slot] = ident % blk_dev
            dest_ref[s, a] = rel * CAP + slot
    for d in range(n_sub):
        for i in range(CAP):
            lists[d][i] = flat_ref[d * CAP + i]


def make_prep(adjacency, n_sub, owner_links, blk_dev):
    int_of = lambda *shape: jax.ShapeDtypeStruct(shape, jnp.int32)
    return pl.pallas_call(
        functools.partial(prep_kernel, owner_links, blk_dev, n_sub),
        in_specs=[SMEM],
        out_specs=[SMEM] * (2 + n_sub),
        out_shape=[int_of(2), int_of(*adjacency.shape)] + [int_of(CAP)] * n_sub,
        scratch_shapes=[pltpu.SMEM((n_sub * CAP,), jnp.int32), pltpu.SMEM((n_sub,), jnp.int32)],
        compiler_params=params(60),
        cost_estimate=cheap(),
        name="prep",
    )(adjacency)


def contrib_kernel(rows_ref, dest_ref, modes_ref, coup_ref, inv_ref, *refs):
    outs, (part_ref, all_ref) = refs[:-2], refs[-2:]
    s = pl.program_id(0)
    links, rows, block = coup_ref.shape[1:]
    live = lax.broadcasted_iota(jnp.int32, (rows, 1), 0) < rows_ref[s]
    modes = jnp.where(live, modes_ref[0], jnp.zeros((), modes_ref.dtype))
    inv = inv_ref[pl.ds(s, 1), :]
    wide = jnp.concatenate([coup_ref[0, a] for a in range(links)], axis=1)
    red = lax.dot_general(
        wide, modes, (((0,), (0,)), ((), ())), preferred_element_type=jnp.float32
    )
    weighted = (red * inv).astype(jnp.bfloat16)
    red_b = red.astype(jnp.bfloat16)
    for a in range(links):
        part = slice(a * block, (a + 1) * block)
        part_ref[a] = lax.dot_general(
            weighted[part], red_b[part], (((1,), (1,)), ((), ())),
            preferred_element_type=jnp.float32,
        ).astype(jnp.bfloat16)
    for a in range(links):
        all_ref[dest_ref[s, a]] = part_ref[a]

    @pl.when(s == pl.num_programs(0) - 1)
    def _():
        for d, out in enumerate(outs):
            out[...] = all_ref[d * CAP:(d + 1) * CAP]


def make_contrib(dest, modes, coupling, inv_eig, sub_rows, n_sub):
    subs, rows, width = modes.shape
    links, block = coupling.shape[1], coupling.shape[3]
    out = jax.ShapeDtypeStruct((CAP, block, block), jnp.bfloat16)
    return pl.pallas_call(
        contrib_kernel,
        grid=(subs,),
        in_specs=[
            SMEM, SMEM,
            pl.BlockSpec((1, rows, width), lambda s: (s, 0, 0)),
            pl.BlockSpec((1, links, rows, block), lambda s: (s, 0, 0, 0)),
            pl.BlockSpec(inv_eig.shape, lambda s: (0, 0)),
        ],
        out_specs=[pl.BlockSpec(out.shape, lambda s: (0, 0, 0))] * n_sub,
        out_shape=[out] * n_sub,
        scratch_shapes=[
            pltpu.VMEM((links, block, block), jnp.bfloat16),
            pltpu.VMEM((n_sub * CAP, block, block), jnp.bfloat16),
        ],
        compiler_params=params(55),
        cost_estimate=cheap(),
        name="contrib",
    )(sub_rows, dest, modes, coupling, inv_eig)


def near_kernel(base_ref, own_at, pair_at, own_ref, pair_ref, total_ref):
    total_ref[:base_ref.shape[0]] = base_ref[...]
    for place, group in ((own_at, own_ref), (pair_at, pair_ref)):
        for i in range(CAP):
            total_ref[place[i]] += group[i].astype(jnp.float32)


def make_near(base, places, groups):
    blk_dev, block = base.shape[:2]
    return pl.pallas_call(
        near_kernel,
        in_specs=[VMEM] + [SMEM] * 2 + [VMEM] * 2,
        out_specs=VMEM,
        out_shape=jax.ShapeDtypeStruct((blk_dev + 1, block, block), jnp.float32),
        compiler_params=params(12),
        cost_estimate=cheap(),
        name="near",
    )(base, *places, *groups)


def far_kernel(count, near_ref, *rest):
    mass_ref, total_ref = rest[-2:]
    total_ref[...] = near_ref[...]
    for place, group in zip(rest[:count], rest[count:2 * count]):
        for i in range(CAP):
            total_ref[place[i]] += group[i].astype(jnp.float32)
    mass_ref[...] = total_ref[:mass_ref.shape[0]].astype(jnp.bfloat16)


def make_far(near, places, groups, behind):
    count, block = near.shape[:2]
    return pl.pallas_call(
        functools.partial(far_kernel, len(groups)),
        in_specs=[VMEM] + [SMEM] * len(places) + [VMEM] * len(groups) + [ANY] * len(behind),
        out_specs=VMEM,
        out_shape=jax.ShapeDtypeStruct((count - 1, block, block), jnp.bfloat16),
        scratch_shapes=[pltpu.VMEM(near.shape, jnp.float32)],
        compiler_params=params(12),
        cost_estimate=cheap(),
        name="far",
    )(near, *places, *groups, *behind)


def turn_kernel(spot_ref, psi_ref, out_ref, copy_ref, sems):
    band, n_sub = out_ref.shape[1], sems.shape[0]

    def bring(j):
        at = pl.ds(pl.multiple_of((spot_ref[0] ^ j) * band, band), band)
        return pltpu.make_async_copy(psi_ref.at[:, at], copy_ref.at[:, at], sems.at[j])

    order = list(range(0, n_sub, CORES)) + [j for j in range(n_sub) if j % CORES]
    for j in order:
        bring(j).start()
    for j in order:
        bring(j).wait()
        if j % CORES == 0:
            at = pl.multiple_of((spot_ref[0] ^ j) * band, band)
            out_ref[j // CORES] = copy_ref[:, pl.ds(at, band)].T


def turn(spot, psi, n_sub):
    depth, width = psi.shape
    shape = (n_sub // CORES, width // n_sub, depth)
    return pl.pallas_call(
        turn_kernel,
        in_specs=[SMEM, ANY],
        out_specs=[VMEM, VMEM],
        out_shape=[
            jax.ShapeDtypeStruct(shape, psi.dtype), jax.ShapeDtypeStruct(psi.shape, psi.dtype)
        ],
        scratch_shapes=[pltpu.SemaphoreType.DMA((n_sub,))],
        compiler_params=params(16),
        cost_estimate=cheap(),
        name="turn",
    )(spot, psi)


def left_kernel(mass_ref, turned_ref, out_ref):
    block = mass_ref.shape[1]
    zero = jnp.zeros((block, block), jnp.bfloat16)
    groups, half, _ = turned_ref.shape
    for j in range(0, mass_ref.shape[0], 2):
        pair = jnp.concatenate(
            [
                jnp.concatenate([mass_ref[j], zero], axis=1),
                jnp.concatenate([zero, mass_ref[j + 1]], axis=1),
            ],
            axis=0,
        )
        cols = slice(j * block, (j + 2) * block)
        out_ref[:, cols] = jnp.dot(
            turned_ref[:, :, cols].reshape(groups * half, 2 * block), pair,
            preferred_element_type=jnp.float32,
        ).astype(jnp.bfloat16)


def make_left(mass, turned):
    groups, half, depth = turned.shape
    return pl.pallas_call(
        left_kernel,
        in_specs=[VMEM, VMEM],
        out_specs=VMEM,
        out_shape=jax.ShapeDtypeStruct((groups * half, depth), jnp.bfloat16),
        compiler_params=params(16),
        cost_estimate=cheap(),
        name="left",
    )(mass, turned)


def product_kernel(chunk, pairs, acc_in, go, keep, behind, spot_ref, *refs):
    lefts, psis, refs = refs[:pairs], refs[pairs:2 * pairs], refs[2 * pairs:]
    acc = refs[0] if acc_in else None
    outs = list(refs[int(acc_in) + behind:])
    high, z = chunk
    core = spot_ref[0] % CORES

    def block(x, y):
        band, width = outs[0].shape[1:]
        rows = pl.ds(pl.multiple_of((2 * high + x) * band, band), band)
        tile = spot_ref[1] ^ (2 * z + y)
        cols = pl.ds(pl.multiple_of(tile * width, width), width)
        res = None
        for left, psi in zip(lefts, psis):
            term = jnp.dot(left[rows], psi[:, cols], preferred_element_type=jnp.float32)
            res = term if res is None else res + term
        return res

    places = []
    if go:
        places += [(outs[0], 0, 1, 1), (outs[0], 1, 1 - core, core)]
    if keep:
        places += [(outs[-1], 0, 0, 0), (outs[-1], 1, core, 1 - core)]
    for out, i, x, y in places:
        res = block(x, y)
        if acc_in:
            res += acc[i]
        out[i] = res.astype(out.dtype)


def product(chunk, spot, lefts, psis, band, width, go=None, keep=False, acc=(), behind=()):
    depth = lefts[0].shape[1]
    types = ([go] if go is not None else []) + ([jnp.float32] if keep else [])
    flops = len(types) * 4 * band * width * depth * len(lefts)
    return pl.pallas_call(
        functools.partial(
            product_kernel, chunk, len(lefts), bool(acc), go is not None, keep, len(behind)
        ),
        in_specs=[SMEM] + [VMEM] * (2 * len(lefts) + len(acc)) + [ANY] * len(behind),
        out_specs=[VMEM] * len(types),
        out_shape=[jax.ShapeDtypeStruct((2, band, width), t) for t in types],
        compiler_params=params(16),
        cost_estimate=pl.CostEstimate(
            flops=flops, bytes_accessed=flops // 512, transcendentals=0
        ),
        name="product",
    )(spot, *lefts, *psis, *acc, *behind)


def first_kernel(keep_ref, got_ref, *refs):
    low_ref, go_ref = refs[-2:]
    low_ref[...] = keep_ref[0] + got_ref[1].astype(jnp.float32)
    go_ref[...] = (keep_ref[1] + got_ref[0].astype(jnp.float32)).astype(jnp.bfloat16)


def add_first(keep, got, behind=()):
    shape = keep.shape[1:]
    return pl.pallas_call(
        first_kernel,
        in_specs=[VMEM] * 2 + [ANY] * len(behind),
        out_specs=[VMEM] * 2,
        out_shape=[jax.ShapeDtypeStruct(shape, t) for t in (jnp.float32, jnp.bfloat16)],
        compiler_params=params(12),
        cost_estimate=cheap(),
        name="add_first",
    )(keep, got, *behind)


def second_kernel(low_ref, got_ref, *refs):
    total = low_ref[...] + got_ref[...].astype(jnp.float32)
    for v in refs[:-1]:
        total += v[...].astype(jnp.float32)
    refs[-1][...] = total.astype(refs[-1].dtype)


def add_second(low, got, dtype, tails=()):
    return pl.pallas_call(
        second_kernel,
        in_specs=[VMEM] * (2 + len(tails)),
        out_specs=VMEM,
        out_shape=jax.ShapeDtypeStruct(low.shape, dtype),
        compiler_params=params(12),
        cost_estimate=cheap(),
        name="add_second",
    )(low, got, *tails)


def on_device(modes, coupling, inv_eig, sub_rows, adjacency, base_mass, iface_modes):
    n_sub = lax.axis_size("sub")
    n_tile = lax.axis_size("tile")
    blk_dev = base_mass.shape[0]
    owner_links = blk_dev * n_tile
    width = iface_modes.shape[1]
    band, tile = width // n_sub, width // n_tile
    def swap_sub(v, d):
        return lax.ppermute(v, "sub", [(i, i ^ d) for i in range(n_sub)])

    def swap(v, partner):
        pairs = []
        for i in range(n_sub):
            for j in range(n_tile):
                k, m = partner(i, j)
                pairs.append((i * n_tile + j, k * n_tile + m))
        return lax.ppermute(v, ("sub", "tile"), pairs)

    def swap_first(v):
        return swap(v, lambda i, j: (i, j ^ 1) if i % CORES else (i ^ CORES, j))

    def swap_second(v):
        return swap(v, lambda i, j: (i ^ CORES, j) if i % CORES else (i, j ^ 1))

    def swap_third(v, chunk):
        high, z = chunk
        bit = z & -z if z else 0
        step = 0 if z else (high & -high) * 2 * CORES
        return swap(v, lambda i, j: (i ^ step, j ^ (2 * bit)))

    spot, dest, *lists = make_prep(adjacency, n_sub, owner_links, blk_dev)
    lists = [swap_sub(v, d) if d else v for d, v in enumerate(lists)]
    other = swap_sub(iface_modes, 1)
    sent = make_contrib(dest, modes, coupling, inv_eig, sub_rows, n_sub)
    far = [swap_sub(sent[d], d) for d in range(CORES, n_sub)]
    near = make_near(base_mass, lists[:CORES], [sent[0], swap_sub(sent[1], 1)])
    own_t, own = turn(spot, iface_modes, n_sub)
    other_t, other = turn(spot, other, n_sub)
    mass = make_far(near, lists[CORES:], far, [own_t, other_t])
    mass_other = swap_sub(mass, 1)
    left = make_left(mass, own_t)

    chunks = [(h, z) for h in range(n_sub // (2 * CORES)) for z in range(n_tile // 2)][::-1]
    goes_to = {(h, z): (h, z & (z - 1)) if z else (h & (h - 1), 0) for h, z in chunks[:-1]}
    head = product(chunks[0], spot, [left], [own], band, tile, go=jnp.float32)
    left_other = make_left(mass_other, other_t)
    lefts, psis = [left, left_other], [own, other]

    keep, first, second, third = {}, {}, {}, []
    tails = {c: [] for c in chunks}
    last = len(chunks) - 1
    for i in range(last + 2):
        if i == 0:
            go, = product(
                chunks[0], spot, [left_other], [other], band, tile, go=jnp.bfloat16, acc=head
            )
            keep[0], = product(
                chunks[0], spot, lefts, psis, band, tile, keep=True, behind=[go]
            )
            first[0] = swap_first(go)
        elif i <= last:
            behind = [keep[0]] if i == 1 else [second[i - 2][0]]
            go, keep[i] = product(
                chunks[i], spot, lefts, psis, band, tile, go=jnp.bfloat16, keep=True,
                behind=behind,
            )
            first[i] = swap_first(go)
        if i > 1:
            chunk = chunks[i - 2]
            third.append(add_second(*second[i - 2], jnp.bfloat16, tails[chunk]))
            tails[goes_to[chunk]].append(swap_third(third[-1], chunk))
        if i:
            low, go = add_first(keep[i - 1], first[i - 1], third[i - 2:])
            second[i - 1] = low, swap_second(go)
    low, got = second[last]
    early, late = tails[chunks[-1]][:-1], tails[chunks[-1]][-1:]
    if early:
        low = add_second(low, early[0], jnp.float32, early[1:])
    return add_second(low, got, jnp.float32, late)


def solution(mesh):
    placed = (
        P(("sub", "tile"), None, None),
        P(("sub", "tile"), None, None, None),
        P(("sub", "tile"), None),
        P(("sub", "tile")),
        P(("sub", "tile"), None),
        P(("sub", "tile"), None, None),
        P(("sub", "tile"), None),
    )
    return jax.shard_map(
        on_device, mesh=mesh, in_specs=placed, out_specs=P("sub", "tile"), check_vma=False
    )
```

```python
import functools

import jax
import jax.numpy as jnp
from jax import lax
from jax.experimental import pallas as pl
from jax.experimental.pallas import tpu as pltpu
from jax.sharding import PartitionSpec as P

CAP = 8
CORES = 2
MIB = 1024 * 1024
SMEM = pl.BlockSpec(memory_space=pltpu.SMEM)
VMEM = pl.BlockSpec(memory_space=pltpu.VMEM)


def params(mib):
    return pltpu.CompilerParams(vmem_limit_bytes=mib * MIB)


def cheap():
    return pl.CostEstimate(flops=1, bytes_accessed=1, transcendentals=0)


ANY = pl.BlockSpec(memory_space=pl.ANY)


def prep_kernel(owner_links, blk_dev, n_sub, adj_ref, spot_ref, dest_ref, *refs):
    lists, (flat_ref, count_ref) = refs[:n_sub], refs[n_sub:]
    sub = lax.axis_index("sub")
    spot_ref[0] = sub
    spot_ref[1] = lax.axis_index("tile")
    subs, links = adj_ref.shape
    for d in range(n_sub):
        count_ref[d] = 0
        for i in range(CAP):
            flat_ref[d * CAP + i] = blk_dev
    for s in range(subs):
        for a in range(links):
            ident = adj_ref[s, a]
            rel = (ident // owner_links) ^ sub
            slot = count_ref[rel]
            count_ref[rel] = slot + 1
            flat_ref[rel * CAP + slot] = ident % blk_dev
            dest_ref[s, a] = rel * CAP + slot
    for d in range(n_sub):
        for i in range(CAP):
            lists[d][i] = flat_ref[d * CAP + i]


def make_prep(adjacency, n_sub, owner_links, blk_dev):
    int_of = lambda *shape: jax.ShapeDtypeStruct(shape, jnp.int32)
    return pl.pallas_call(
        functools.partial(prep_kernel, owner_links, blk_dev, n_sub),
        in_specs=[SMEM],
        out_specs=[SMEM] * (2 + n_sub),
        out_shape=[int_of(2), int_of(*adjacency.shape)] + [int_of(CAP)] * n_sub,
        scratch_shapes=[pltpu.SMEM((n_sub * CAP,), jnp.int32), pltpu.SMEM((n_sub,), jnp.int32)],
        compiler_params=params(60),
        cost_estimate=cheap(),
        name="prep",
    )(adjacency)


def contrib_kernel(rows_ref, dest_ref, modes_ref, coup_ref, inv_ref, *refs):
    outs, (part_ref, all_ref) = refs[:-2], refs[-2:]
    s = pl.program_id(0)
    links, rows, block = coup_ref.shape[1:]
    live = lax.broadcasted_iota(jnp.int32, (rows, 1), 0) < rows_ref[s]
    modes = jnp.where(live, modes_ref[0], jnp.zeros((), modes_ref.dtype))
    inv = inv_ref[pl.ds(s, 1), :]
    wide = jnp.concatenate([coup_ref[0, a] for a in range(links)], axis=1)
    red = lax.dot_general(
        wide, modes, (((0,), (0,)), ((), ())), preferred_element_type=jnp.float32
    )
    weighted = (red * inv).astype(jnp.bfloat16)
    red_b = red.astype(jnp.bfloat16)
    for a in range(links):
        part = slice(a * block, (a + 1) * block)
        part_ref[a] = lax.dot_general(
            weighted[part], red_b[part], (((1,), (1,)), ((), ())),
            preferred_element_type=jnp.float32,
        ).astype(jnp.bfloat16)
    for a in range(links):
        all_ref[dest_ref[s, a]] = part_ref[a]

    @pl.when(s == pl.num_programs(0) - 1)
    def _():
        for d, out in enumerate(outs):
            out[...] = all_ref[d * CAP:(d + 1) * CAP]


def make_contrib(dest, modes, coupling, inv_eig, sub_rows, n_sub):
    subs, rows, width = modes.shape
    links, block = coupling.shape[1], coupling.shape[3]
    out = jax.ShapeDtypeStruct((CAP, block, block), jnp.bfloat16)
    return pl.pallas_call(
        contrib_kernel,
        grid=(subs,),
        in_specs=[
            SMEM, SMEM,
            pl.BlockSpec((1, rows, width), lambda s: (s, 0, 0)),
            pl.BlockSpec((1, links, rows, block), lambda s: (s, 0, 0, 0)),
            pl.BlockSpec(inv_eig.shape, lambda s: (0, 0)),
        ],
        out_specs=[pl.BlockSpec(out.shape, lambda s: (0, 0, 0))] * n_sub,
        out_shape=[out] * n_sub,
        scratch_shapes=[
            pltpu.VMEM((links, block, block), jnp.bfloat16),
            pltpu.VMEM((n_sub * CAP, block, block), jnp.bfloat16),
        ],
        compiler_params=params(55),
        cost_estimate=cheap(),
        name="contrib",
    )(sub_rows, dest, modes, coupling, inv_eig)


def near_kernel(base_ref, own_at, pair_at, own_ref, pair_ref, total_ref):
    total_ref[:base_ref.shape[0]] = base_ref[...]
    for place, group in ((own_at, own_ref), (pair_at, pair_ref)):
        for i in range(CAP):
            total_ref[place[i]] += group[i].astype(jnp.float32)


def make_near(base, places, groups):
    blk_dev, block = base.shape[:2]
    return pl.pallas_call(
        near_kernel,
        in_specs=[VMEM] + [SMEM] * 2 + [VMEM] * 2,
        out_specs=VMEM,
        out_shape=jax.ShapeDtypeStruct((blk_dev + 1, block, block), jnp.float32),
        compiler_params=params(12),
        cost_estimate=cheap(),
        name="near",
    )(base, *places, *groups)


def far_kernel(count, near_ref, *rest):
    mass_ref, total_ref = rest[-2:]
    total_ref[...] = near_ref[...]
    for place, group in zip(rest[:count], rest[count:2 * count]):
        for i in range(CAP):
            total_ref[place[i]] += group[i].astype(jnp.float32)
    mass_ref[...] = total_ref[:mass_ref.shape[0]].astype(jnp.bfloat16)


def make_far(near, places, groups, behind):
    count, block = near.shape[:2]
    return pl.pallas_call(
        functools.partial(far_kernel, len(groups)),
        in_specs=[VMEM] + [SMEM] * len(places) + [VMEM] * len(groups) + [ANY] * len(behind),
        out_specs=VMEM,
        out_shape=jax.ShapeDtypeStruct((count - 1, block, block), jnp.bfloat16),
        scratch_shapes=[pltpu.VMEM(near.shape, jnp.float32)],
        compiler_params=params(12),
        cost_estimate=cheap(),
        name="far",
    )(near, *places, *groups, *behind)


def turn_kernel(spot_ref, psi_ref, out_ref, copy_ref, sems):
    band, n_sub = out_ref.shape[1], sems.shape[0]

    def bring(j):
        at = pl.ds(pl.multiple_of((spot_ref[0] ^ j) * band, band), band)
        return pltpu.make_async_copy(psi_ref.at[:, at], copy_ref.at[:, at], sems.at[j])

    order = list(range(0, n_sub, CORES)) + [j for j in range(n_sub) if j % CORES]
    for j in order:
        bring(j).start()
    for j in order:
        bring(j).wait()
        if j % CORES == 0:
            at = pl.multiple_of((spot_ref[0] ^ j) * band, band)
            out_ref[j // CORES] = copy_ref[:, pl.ds(at, band)].T


def turn(spot, psi, n_sub):
    depth, width = psi.shape
    shape = (n_sub // CORES, width // n_sub, depth)
    return pl.pallas_call(
        turn_kernel,
        in_specs=[SMEM, ANY],
        out_specs=[VMEM, VMEM],
        out_shape=[
            jax.ShapeDtypeStruct(shape, psi.dtype), jax.ShapeDtypeStruct(psi.shape, psi.dtype)
        ],
        scratch_shapes=[pltpu.SemaphoreType.DMA((n_sub,))],
        compiler_params=params(16),
        cost_estimate=cheap(),
        name="turn",
    )(spot, psi)


def left_kernel(mass_ref, turned_ref, out_ref):
    block = mass_ref.shape[1]
    zero = jnp.zeros((block, block), jnp.bfloat16)
    groups, half, _ = turned_ref.shape
    for j in range(0, mass_ref.shape[0], 2):
        pair = jnp.concatenate(
            [
                jnp.concatenate([mass_ref[j], zero], axis=1),
                jnp.concatenate([zero, mass_ref[j + 1]], axis=1),
            ],
            axis=0,
        )
        cols = slice(j * block, (j + 2) * block)
        out_ref[:, cols] = jnp.dot(
            turned_ref[:, :, cols].reshape(groups * half, 2 * block), pair,
            preferred_element_type=jnp.float32,
        ).astype(jnp.bfloat16)


def make_left(mass, turned):
    groups, half, depth = turned.shape
    return pl.pallas_call(
        left_kernel,
        in_specs=[VMEM, VMEM],
        out_specs=VMEM,
        out_shape=jax.ShapeDtypeStruct((groups * half, depth), jnp.bfloat16),
        compiler_params=params(16),
        cost_estimate=cheap(),
        name="left",
    )(mass, turned)


def product_kernel(chunk, pairs, acc_in, go, keep, behind, spot_ref, *refs):
    lefts, psis, refs = refs[:pairs], refs[pairs:2 * pairs], refs[2 * pairs:]
    acc = refs[0] if acc_in else None
    outs = list(refs[int(acc_in) + behind:])
    high, z = chunk
    core = spot_ref[0] % CORES

    def block(x, y):
        band, width = outs[0].shape[1:]
        rows = pl.ds(pl.multiple_of((2 * high + x) * band, band), band)
        tile = spot_ref[1] ^ (2 * z + y)
        cols = pl.ds(pl.multiple_of(tile * width, width), width)
        res = None
        for left, psi in zip(lefts, psis):
            term = jnp.dot(left[rows], psi[:, cols], preferred_element_type=jnp.float32)
            res = term if res is None else res + term
        return res

    places = []
    if go:
        places += [(outs[0], 0, 1, 1), (outs[0], 1, 1 - core, core)]
    if keep:
        places += [(outs[-1], 0, 0, 0), (outs[-1], 1, core, 1 - core)]
    for out, i, x, y in places:
        res = block(x, y)
        if acc_in:
            res += acc[i]
        out[i] = res.astype(out.dtype)


def product(chunk, spot, lefts, psis, band, width, go=None, keep=False, acc=(), behind=()):
    depth = lefts[0].shape[1]
    types = ([go] if go is not None else []) + ([jnp.float32] if keep else [])
    flops = len(types) * 4 * band * width * depth * len(lefts)
    return pl.pallas_call(
        functools.partial(
            product_kernel, chunk, len(lefts), bool(acc), go is not None, keep, len(behind)
        ),
        in_specs=[SMEM] + [VMEM] * (2 * len(lefts) + len(acc)) + [ANY] * len(behind),
        out_specs=[VMEM] * len(types),
        out_shape=[jax.ShapeDtypeStruct((2, band, width), t) for t in types],
        compiler_params=params(16),
        cost_estimate=pl.CostEstimate(
            flops=flops, bytes_accessed=flops // 512, transcendentals=0
        ),
        name="product",
    )(spot, *lefts, *psis, *acc, *behind)


def first_kernel(keep_ref, got_ref, *refs):
    low_ref, go_ref = refs[-2:]
    low_ref[...] = keep_ref[0] + got_ref[1].astype(jnp.float32)
    go_ref[...] = (keep_ref[1] + got_ref[0].astype(jnp.float32)).astype(jnp.bfloat16)


def add_first(keep, got, behind=()):
    shape = keep.shape[1:]
    return pl.pallas_call(
        first_kernel,
        in_specs=[VMEM] * 2 + [ANY] * len(behind),
        out_specs=[VMEM] * 2,
        out_shape=[jax.ShapeDtypeStruct(shape, t) for t in (jnp.float32, jnp.bfloat16)],
        compiler_params=params(12),
        cost_estimate=cheap(),
        name="add_first",
    )(keep, got, *behind)


def second_kernel(low_ref, got_ref, *refs):
    total = low_ref[...] + got_ref[...].astype(jnp.float32)
    for v in refs[:-1]:
        total += v[...].astype(jnp.float32)
    refs[-1][...] = total.astype(refs[-1].dtype)


def add_second(low, got, dtype, tails=()):
    return pl.pallas_call(
        second_kernel,
        in_specs=[VMEM] * (2 + len(tails)),
        out_specs=VMEM,
        out_shape=jax.ShapeDtypeStruct(low.shape, dtype),
        compiler_params=params(12),
        cost_estimate=cheap(),
        name="add_second",
    )(low, got, *tails)


def on_device(modes, coupling, inv_eig, sub_rows, adjacency, base_mass, iface_modes):
    n_sub = lax.axis_size("sub")
    n_tile = lax.axis_size("tile")
    blk_dev = base_mass.shape[0]
    owner_links = blk_dev * n_tile
    width = iface_modes.shape[1]
    band, tile = width // n_sub, width // n_tile
    def swap_sub(v, d):
        return lax.ppermute(v, "sub", [(i, i ^ d) for i in range(n_sub)])

    def swap(v, partner):
        pairs = []
        for i in range(n_sub):
            for j in range(n_tile):
                k, m = partner(i, j)
                pairs.append((i * n_tile + j, k * n_tile + m))
        return lax.ppermute(v, ("sub", "tile"), pairs)

    def swap_first(v):
        return swap(v, lambda i, j: (i, j ^ 1) if i % CORES else (i ^ CORES, j))

    def swap_second(v):
        return swap(v, lambda i, j: (i ^ CORES, j) if i % CORES else (i, j ^ 1))

    def swap_third(v, chunk):
        high, z = chunk
        bit = z & -z if z else 0
        step = 0 if z else (high & -high) * 2 * CORES
        return swap(v, lambda i, j: (i ^ step, j ^ (2 * bit)))

    spot, dest, *lists = make_prep(adjacency, n_sub, owner_links, blk_dev)
    lists = [swap_sub(v, d) if d else v for d, v in enumerate(lists)]
    other = swap_sub(iface_modes, 1)
    sent = make_contrib(dest, modes, coupling, inv_eig, sub_rows, n_sub)
    far = [swap_sub(sent[d], d) for d in range(CORES, n_sub)]
    near = make_near(base_mass, lists[:CORES], [sent[0], swap_sub(sent[1], 1)])
    own_t, own = turn(spot, iface_modes, n_sub)
    other_t, other = turn(spot, other, n_sub)
    mass = make_far(near, lists[CORES:], far, [own_t, other_t])
    mass_other = swap_sub(mass, 1)
    left = make_left(mass, own_t)

    chunks = [(h, z) for h in range(n_sub // (2 * CORES)) for z in range(n_tile // 2)][::-1]
    goes_to = {(h, z): (h, z & (z - 1)) if z else (h & (h - 1), 0) for h, z in chunks[:-1]}
    head = product(chunks[0], spot, [left], [own], band, tile, go=jnp.float32)
    left_other = make_left(mass_other, other_t)
    lefts, psis = [left, left_other], [own, other]

    keep, first, second, third = {}, {}, {}, {}
    tails = {c: [] for c in chunks}
    last = len(chunks) - 1
    common = spot, lefts, psis, band, tile
    go, = product(
        chunks[0], spot, [left_other], [other], band, tile, go=jnp.bfloat16, acc=head
    )
    for i in range(last + 1):
        first[i] = swap_first(go)
        if i < last:
            behind = [second[i - 1][0]] if i else [go]
            go, = product(chunks[i + 1], *common, go=jnp.bfloat16, behind=behind)
        behind = [go] + ([third[i - 2]] if i - 2 in third else [])
        keep[i], = product(chunks[i], *common, keep=True, behind=behind)
        behind = [third[i - 2]] if 0 and i > 1 else []
        low, move = add_first(keep[i], first[i], behind)
        second[i] = low, swap_second(move)
        if i:
            chunk = chunks[i - 1]
            third[i - 1] = add_second(*second[i - 1], jnp.bfloat16, tails[chunk])
            tails[goes_to[chunk]].append(swap_third(third[i - 1], chunk))
    low, got = second[last]
    early, late = tails[chunks[-1]], []
    if early:
        low = add_second(low, early[0], jnp.float32, early[1:])
    return add_second(low, got, jnp.float32, late)


def solution(mesh):
    placed = (
        P(("sub", "tile"), None, None),
        P(("sub", "tile"), None, None, None),
        P(("sub", "tile"), None),
        P(("sub", "tile")),
        P(("sub", "tile"), None),
        P(("sub", "tile"), None, None),
        P(("sub", "tile"), None),
    )
    return jax.shard_map(
        on_device, mesh=mesh, in_specs=placed, out_specs=P("sub", "tile"), check_vma=False
    )
```

```python
import functools

import jax
import jax.numpy as jnp
from jax import lax
from jax.experimental import pallas as pl
from jax.experimental.pallas import tpu as pltpu
from jax.sharding import PartitionSpec as P

CAP = 8
TAIL = 16
CORES = 2
MIB = 1024 * 1024
SMEM = pl.BlockSpec(memory_space=pltpu.SMEM)
VMEM = pl.BlockSpec(memory_space=pltpu.VMEM)


def params(mib):
    return pltpu.CompilerParams(vmem_limit_bytes=mib * MIB)


def cheap():
    return pl.CostEstimate(flops=1, bytes_accessed=1, transcendentals=0)


ANY = pl.BlockSpec(memory_space=pl.ANY)


def corner(block):
    row = lax.broadcasted_iota(jnp.int32, (block // 2, block), 0)
    return row, lax.broadcasted_iota(jnp.int32, (block // 2, block), 1)


def pack(square):
    block = square.shape[0]
    half = block // 2
    row, lane = corner(block)
    last = pltpu.roll(square[half:], half, 1)
    upper = jnp.where(lane < row, last, square[:half])
    diagonal = jnp.sum(jnp.where(lane == row, last, 0.0), axis=0, keepdims=True)
    return upper.astype(jnp.bfloat16), diagonal


def unpack(upper, diagonal):
    block = upper.shape[1]
    half = block // 2
    row, lane = corner(block)
    top = jnp.where(lane > row, upper, jnp.where(lane == row, 0.5 * upper, 0.0))
    low = jnp.where(lane < row, upper, jnp.where(lane == row, 0.5 * diagonal, 0.0))
    square = jnp.concatenate([top, pltpu.roll(low, half, 1)], axis=0)
    return square + square.T


def contrib_kernel(
    owner_links, blk_dev, n_sub, rows_ref, adj_ref, modes_ref, coup_ref, inv_ref, *refs
):
    outs = refs[:n_sub]
    part_ref, edge_ref, all_ref, side_ref, count_ref, local_ref = refs[n_sub:]
    s = pl.program_id(0)
    sub = lax.axis_index("sub")
    links, rows, block = coup_ref.shape[1:]

    @pl.when(s == 0)
    def _():
        for d in range(n_sub):
            count_ref[d] = 0
            for i in range(CAP):
                local_ref[d * CAP + i] = blk_dev

    live = lax.broadcasted_iota(jnp.int32, (rows, 1), 0) < rows_ref[s]
    modes = jnp.where(live, modes_ref[0], jnp.zeros((), modes_ref.dtype))
    inv = inv_ref[pl.ds(s, 1), :]
    wide = jnp.concatenate([coup_ref[0, a] for a in range(links)], axis=1)
    red = lax.dot_general(
        wide, modes, (((0,), (0,)), ((), ())), preferred_element_type=jnp.float32
    )
    weighted = (red * inv).astype(jnp.bfloat16)
    red_b = red.astype(jnp.bfloat16)
    group = 2 if links % 2 == 0 else 1
    for a in range(0, links, group):
        part = slice(a * block, (a + group) * block)
        square = lax.dot_general(
            weighted[part], red_b[part], (((1,), (1,)), ((), ())),
            preferred_element_type=jnp.float32,
        )
        for i in range(group):
            here = slice(i * block, (i + 1) * block)
            upper, diagonal = pack(square[here, here])
            part_ref[a + i] = upper
            edge_ref[a + i] = diagonal
    for a in range(links):
        ident = adj_ref[s, a]
        rel = (ident // owner_links) ^ sub
        slot = count_ref[rel]
        count_ref[rel] = slot + 1
        at = rel * CAP + slot
        local_ref[at] = ident % blk_dev
        all_ref[at] = part_ref[a]
        side_ref[at] = edge_ref[a]

    @pl.when(s == pl.num_programs(0) - 1)
    def _():
        half = block // 2
        row = lax.broadcasted_iota(jnp.int32, (TAIL, block), 0)
        lane = lax.broadcasted_iota(jnp.int32, (TAIL, block), 1)
        for d, out in enumerate(outs):
            tail = jnp.zeros((TAIL, block), jnp.float32)
            for i in range(CAP):
                out[i * half:(i + 1) * half] = all_ref[d * CAP + i]
                place = local_ref[d * CAP + i].astype(jnp.float32)
                tail = jnp.where(
                    row == i, jnp.where(lane < half, side_ref[d * CAP + i], place), tail
                )
            out[CAP * half:] = tail.astype(jnp.bfloat16)


def make_contrib(modes, coupling, inv_eig, sub_rows, adjacency, n_sub, owner_links, blk_dev):
    subs, rows, width = modes.shape
    links, block = coupling.shape[1], coupling.shape[3]
    out = jax.ShapeDtypeStruct((CAP * block // 2 + TAIL, block), jnp.bfloat16)
    return pl.pallas_call(
        functools.partial(contrib_kernel, owner_links, blk_dev, n_sub),
        grid=(subs,),
        in_specs=[
            SMEM, SMEM,
            pl.BlockSpec((1, rows, width), lambda s: (s, 0, 0)),
            pl.BlockSpec((1, links, rows, block), lambda s: (s, 0, 0, 0)),
            pl.BlockSpec(inv_eig.shape, lambda s: (0, 0)),
        ],
        out_specs=[pl.BlockSpec(out.shape, lambda s: (0, 0))] * n_sub,
        out_shape=[out] * n_sub,
        scratch_shapes=[
            pltpu.VMEM((links, block // 2, block), jnp.bfloat16),
            pltpu.VMEM((links, 1, block), jnp.float32),
            pltpu.VMEM((n_sub * CAP, block // 2, block), jnp.bfloat16),
            pltpu.VMEM((n_sub * CAP, 1, block), jnp.float32),
            pltpu.SMEM((n_sub,), jnp.int32),
            pltpu.SMEM((n_sub * CAP,), jnp.int32),
        ],
        compiler_params=params(55),
        cost_estimate=cheap(),
        name="contrib",
    )(sub_rows, adjacency, modes, coupling, inv_eig)


def add_groups(upper_ref, side_ref, groups):
    half, block = upper_ref.shape[1:]
    for group in groups:
        tail = group[CAP * half:].astype(jnp.float32)
        for i in range(CAP):
            place = jnp.max(tail[i:i + 1, half:]).astype(jnp.int32)
            upper_ref[place] += group[i * half:(i + 1) * half].astype(jnp.float32)
            side_ref[place] += tail[i:i + 1]


def near_kernel(own_ref, pair_ref, upper_ref, side_ref):
    upper_ref[...] = jnp.zeros_like(upper_ref)
    side_ref[...] = jnp.zeros_like(side_ref)
    add_groups(upper_ref, side_ref, (own_ref, pair_ref))


def make_near(blk_dev, groups):
    block = groups[0].shape[1]
    shapes = [(blk_dev + 1, block // 2, block), (blk_dev + 1, 1, block)]
    return pl.pallas_call(
        near_kernel,
        in_specs=[VMEM] * 2,
        out_specs=[VMEM] * 2,
        out_shape=[jax.ShapeDtypeStruct(v, jnp.float32) for v in shapes],
        compiler_params=params(12),
        cost_estimate=cheap(),
        name="near",
    )(*groups)


def far_kernel(count, base_ref, near_ref, near_side_ref, *rest):
    mass_ref, upper_ref, side_ref = rest[-3:]
    upper_ref[...] = near_ref[...]
    side_ref[...] = near_side_ref[...]
    add_groups(upper_ref, side_ref, rest[:count])
    for b in range(mass_ref.shape[0]):
        mass_ref[b] = (base_ref[b] + unpack(upper_ref[b], side_ref[b])).astype(jnp.bfloat16)


def make_far(base, near, groups, behind):
    return pl.pallas_call(
        functools.partial(far_kernel, len(groups)),
        in_specs=[VMEM] * (3 + len(groups)) + [ANY] * len(behind),
        out_specs=VMEM,
        out_shape=jax.ShapeDtypeStruct(base.shape, jnp.bfloat16),
        scratch_shapes=[pltpu.VMEM(v.shape, jnp.float32) for v in near],
        compiler_params=params(12),
        cost_estimate=cheap(),
        name="far",
    )(base, *near, *groups, *behind)


def turn_kernel(psi_ref, out_ref, copy_ref, sems):
    band, n_sub = out_ref.shape[1], sems.shape[0]

    def bring(j):
        at = pl.ds(pl.multiple_of((lax.axis_index("sub") ^ j) * band, band), band)
        return pltpu.make_async_copy(psi_ref.at[:, at], copy_ref.at[:, at], sems.at[j])

    order = list(range(0, n_sub, CORES)) + [j for j in range(n_sub) if j % CORES]
    for j in order:
        bring(j).start()
    for j in order:
        bring(j).wait()
        if j % CORES == 0:
            at = pl.multiple_of((lax.axis_index("sub") ^ j) * band, band)
            out_ref[j // CORES] = copy_ref[:, pl.ds(at, band)].T


def turn(psi, n_sub):
    depth, width = psi.shape
    shape = (n_sub // CORES, width // n_sub, depth)
    return pl.pallas_call(
        turn_kernel,
        in_specs=[ANY],
        out_specs=[VMEM, VMEM],
        out_shape=[
            jax.ShapeDtypeStruct(shape, psi.dtype), jax.ShapeDtypeStruct(psi.shape, psi.dtype)
        ],
        scratch_shapes=[pltpu.SemaphoreType.DMA((n_sub,))],
        compiler_params=params(16),
        cost_estimate=cheap(),
        name="turn",
    )(psi)


def turn_own_kernel(psi_ref, out_ref):
    n_x, band = out_ref.shape[:2]
    for x in range(n_x):
        at = pl.multiple_of((lax.axis_index("sub") ^ (x * CORES)) * band, band)
        out_ref[x] = psi_ref[:, pl.ds(at, band)].T


def turn_own(psi, n_sub):
    depth, width = psi.shape
    return pl.pallas_call(
        turn_own_kernel,
        in_specs=[VMEM],
        out_specs=VMEM,
        out_shape=jax.ShapeDtypeStruct((n_sub // CORES, width // n_sub, depth), psi.dtype),
        compiler_params=params(16),
        cost_estimate=cheap(),
        name="turn_own",
    )(psi)


def left_kernel(mass_ref, turned_ref, out_ref):
    block = mass_ref.shape[1]
    zero = jnp.zeros((block, block), jnp.bfloat16)
    groups, half, _ = turned_ref.shape
    for j in range(0, mass_ref.shape[0], 2):
        pair = jnp.concatenate(
            [
                jnp.concatenate([mass_ref[j], zero], axis=1),
                jnp.concatenate([zero, mass_ref[j + 1]], axis=1),
            ],
            axis=0,
        )
        cols = slice(j * block, (j + 2) * block)
        out_ref[:, cols] = jnp.dot(
            turned_ref[:, :, cols].reshape(groups * half, 2 * block), pair,
            preferred_element_type=jnp.float32,
        ).astype(jnp.bfloat16)


def make_left(mass, turned):
    groups, half, depth = turned.shape
    return pl.pallas_call(
        left_kernel,
        in_specs=[VMEM, VMEM],
        out_specs=VMEM,
        out_shape=jax.ShapeDtypeStruct((groups * half, depth), jnp.bfloat16),
        compiler_params=params(16),
        cost_estimate=cheap(),
        name="left",
    )(mass, turned)


def product_kernel(chunk, pairs, acc_in, go, keep, behind, *refs):
    lefts, psis, refs = refs[:pairs], refs[pairs:2 * pairs], refs[2 * pairs:]
    acc = refs[0] if acc_in else None
    outs = list(refs[int(acc_in) + behind:])
    high, z = chunk
    core = lax.axis_index("sub") % CORES

    def block(x, y):
        band, width = outs[0].shape[1:]
        rows = pl.ds(pl.multiple_of((2 * high + x) * band, band), band)
        tile = lax.axis_index("tile") ^ (2 * z + y)
        cols = pl.ds(pl.multiple_of(tile * width, width), width)
        res = None
        for left, psi in zip(lefts, psis):
            term = jnp.dot(left[rows], psi[:, cols], preferred_element_type=jnp.float32)
            res = term if res is None else res + term
        return res

    places = []
    if go:
        places += [(outs[0], 0, 1, 1), (outs[0], 1, 1 - core, core)]
    if keep:
        places += [(outs[-1], 0, 0, 0), (outs[-1], 1, core, 1 - core)]
    for out, i, x, y in places:
        res = block(x, y)
        if acc_in:
            res += acc[i]
        out[i] = res.astype(out.dtype)


def product(chunk, lefts, psis, band, width, go=None, keep=False, acc=(), behind=()):
    depth = lefts[0].shape[1]
    types = ([go] if go is not None else []) + ([jnp.float32] if keep else [])
    flops = len(types) * 4 * band * width * depth * len(lefts)
    return pl.pallas_call(
        functools.partial(
            product_kernel, chunk, len(lefts), bool(acc), go is not None, keep, len(behind)
        ),
        in_specs=[VMEM] * (2 * len(lefts) + len(acc)) + [ANY] * len(behind),
        out_specs=[VMEM] * len(types),
        out_shape=[jax.ShapeDtypeStruct((2, band, width), t) for t in types],
        compiler_params=params(16),
        cost_estimate=pl.CostEstimate(
            flops=flops, bytes_accessed=flops // 512, transcendentals=0
        ),
        name="product",
    )(*lefts, *psis, *acc, *behind)


def first_kernel(keep_ref, got_ref, *refs):
    low_ref, go_ref = refs[-2:]
    low_ref[...] = keep_ref[0] + got_ref[1].astype(jnp.float32)
    go_ref[...] = (keep_ref[1] + got_ref[0].astype(jnp.float32)).astype(jnp.bfloat16)


def add_first(keep, got, behind=()):
    shape = keep.shape[1:]
    return pl.pallas_call(
        first_kernel,
        in_specs=[VMEM] * 2 + [ANY] * len(behind),
        out_specs=[VMEM] * 2,
        out_shape=[jax.ShapeDtypeStruct(shape, t) for t in (jnp.float32, jnp.bfloat16)],
        compiler_params=params(12),
        cost_estimate=cheap(),
        name="add_first",
    )(keep, got, *behind)


def second_kernel(low_ref, got_ref, *refs):
    total = low_ref[...] + got_ref[...].astype(jnp.float32)
    for v in refs[:-1]:
        total += v[...].astype(jnp.float32)
    refs[-1][...] = total.astype(refs[-1].dtype)


def add_second(low, got, dtype, tails=()):
    return pl.pallas_call(
        second_kernel,
        in_specs=[VMEM] * (2 + len(tails)),
        out_specs=VMEM,
        out_shape=jax.ShapeDtypeStruct(low.shape, dtype),
        compiler_params=params(12),
        cost_estimate=cheap(),
        name="add_second",
    )(low, got, *tails)


def on_device(modes, coupling, inv_eig, sub_rows, adjacency, base_mass, iface_modes):
    n_sub = lax.axis_size("sub")
    n_tile = lax.axis_size("tile")
    blk_dev = base_mass.shape[0]
    owner_links = blk_dev * n_tile
    width = iface_modes.shape[1]
    band, tile = width // n_sub, width // n_tile
    def swap_sub(v, d):
        return lax.ppermute(v, "sub", [(i, i ^ d) for i in range(n_sub)])

    def swap(v, partner):
        pairs = []
        for i in range(n_sub):
            for j in range(n_tile):
                k, m = partner(i, j)
                pairs.append((i * n_tile + j, k * n_tile + m))
        return lax.ppermute(v, ("sub", "tile"), pairs)

    def swap_first(v):
        return swap(v, lambda i, j: (i, j ^ 1) if i % CORES else (i ^ CORES, j))

    def swap_second(v):
        return swap(v, lambda i, j: (i ^ CORES, j) if i % CORES else (i, j ^ 1))

    def swap_third(v, chunk):
        high, z = chunk
        bit = z & -z if z else 0
        step = 0 if z else (high & -high) * 2 * CORES
        return swap(v, lambda i, j: (i ^ step, j ^ (2 * bit)))

    other = swap_sub(iface_modes, 1)
    sent = make_contrib(
        modes, coupling, inv_eig, sub_rows, adjacency, n_sub, owner_links, blk_dev
    )
    far = [swap_sub(sent[d], d) for d in range(CORES, n_sub)]
    near = make_near(blk_dev, [sent[0], swap_sub(sent[1], 1)])
    own_t, own = turn_own(iface_modes, n_sub), iface_modes
    other_t, other = turn(other, n_sub)
    mass = make_far(base_mass, near, far, [own_t, other_t])
    mass_other = swap_sub(mass, 1)
    left = make_left(mass, own_t)

    chunks = [(h, z) for h in range(n_sub // (2 * CORES)) for z in range(n_tile // 2)][::-1]
    goes_to = {(h, z): (h, z & (z - 1)) if z else (h & (h - 1), 0) for h, z in chunks[:-1]}
    head = product(chunks[0], [left], [own], band, tile, go=jnp.float32)
    left_other = make_left(mass_other, other_t)
    lefts, psis = [left, left_other], [own, other]

    keep, first, second, third = {}, {}, {}, {}
    tails = {c: [] for c in chunks}
    last = len(chunks) - 1
    common = lefts, psis, band, tile
    go, = product(
        chunks[0], [left_other], [other], band, tile, go=jnp.bfloat16, acc=head
    )
    for i in range(last + 1):
        first[i] = swap_first(go)
        if i < last:
            behind = [second[i - 1][0]] if i else [go]
            go, = product(chunks[i + 1], *common, go=jnp.bfloat16, behind=behind)
        behind = [go] + ([third[i - 2]] if i - 2 in third else [])
        keep[i], = product(chunks[i], *common, keep=True, behind=behind)
        behind = [third[i - 2]] if 0 and i > 1 else []
        low, move = add_first(keep[i], first[i], behind)
        second[i] = low, swap_second(move)
        if i:
            chunk = chunks[i - 1]
            third[i - 1] = add_second(*second[i - 1], jnp.bfloat16, tails[chunk])
            tails[goes_to[chunk]].append(swap_third(third[i - 1], chunk))
    low, got = second[last]
    early, late = tails[chunks[-1]], []
    if early:
        low = add_second(low, early[0], jnp.float32, early[1:])
    return add_second(low, got, jnp.float32, late)


def solution(mesh):
    placed = (
        P(("sub", "tile"), None, None),
        P(("sub", "tile"), None, None, None),
        P(("sub", "tile"), None),
        P(("sub", "tile")),
        P(("sub", "tile"), None),
        P(("sub", "tile"), None, None),
        P(("sub", "tile"), None),
    )
    return jax.shard_map(
        on_device, mesh=mesh, in_specs=placed, out_specs=P("sub", "tile"), check_vma=False
    )
```

```python
import functools

import jax
import jax.numpy as jnp
from jax import lax
from jax.experimental import pallas as pl
from jax.experimental.pallas import tpu as pltpu
from jax.sharding import PartitionSpec as P

CAP = 8
TAIL = 16
CORES = 2
MIB = 1024 * 1024
SMEM = pl.BlockSpec(memory_space=pltpu.SMEM)
VMEM = pl.BlockSpec(memory_space=pltpu.VMEM)


def params(mib):
    return pltpu.CompilerParams(vmem_limit_bytes=mib * MIB)


def cheap():
    return pl.CostEstimate(flops=1, bytes_accessed=1, transcendentals=0)


ANY = pl.BlockSpec(memory_space=pl.ANY)


def corner(block):
    row = lax.broadcasted_iota(jnp.int32, (block // 2, block), 0)
    return row, lax.broadcasted_iota(jnp.int32, (block // 2, block), 1)


def pack(square):
    block = square.shape[0]
    half = block // 2
    row, lane = corner(block)
    last = pltpu.roll(square[half:], half, 1)
    upper = jnp.where(lane < row, last, square[:half])
    diagonal = jnp.sum(jnp.where(lane == row, last, 0.0), axis=0, keepdims=True)
    return upper.astype(jnp.bfloat16), diagonal


def unpack(upper, diagonal):
    block = upper.shape[1]
    half = block // 2
    row, lane = corner(block)
    top = jnp.where(lane > row, upper, jnp.where(lane == row, 0.5 * upper, 0.0))
    low = jnp.where(lane < row, upper, jnp.where(lane == row, 0.5 * diagonal, 0.0))
    square = jnp.concatenate([top, pltpu.roll(low, half, 1)], axis=0)
    return square + square.T


def contrib_kernel(
    owner_links, blk_dev, n_sub, rows_ref, adj_ref, modes_ref, coup_ref, inv_ref, *refs
):
    outs = refs[:n_sub]
    part_ref, edge_ref, all_ref, side_ref, count_ref, local_ref = refs[n_sub:]
    s = pl.program_id(0)
    sub = lax.axis_index("sub")
    links, rows, block = coup_ref.shape[1:]

    @pl.when(s == 0)
    def _():
        for d in range(n_sub):
            count_ref[d] = 0
            for i in range(CAP):
                local_ref[d * CAP + i] = blk_dev

    live = lax.broadcasted_iota(jnp.int32, (rows, 1), 0) < rows_ref[s]
    modes = jnp.where(live, modes_ref[0], jnp.zeros((), modes_ref.dtype))
    inv = inv_ref[pl.ds(s, 1), :]
    wide = jnp.concatenate([coup_ref[0, a] for a in range(links)], axis=1)
    red = lax.dot_general(
        wide, modes, (((0,), (0,)), ((), ())), preferred_element_type=jnp.float32
    )
    weighted = (red * inv).astype(jnp.bfloat16)
    red_b = red.astype(jnp.bfloat16)
    group = 2 if links % 2 == 0 else 1
    for a in range(0, links, group):
        part = slice(a * block, (a + group) * block)
        square = lax.dot_general(
            weighted[part], red_b[part], (((1,), (1,)), ((), ())),
            preferred_element_type=jnp.float32,
        )
        for i in range(group):
            here = slice(i * block, (i + 1) * block)
            upper, diagonal = pack(square[here, here])
            part_ref[a + i] = upper
            edge_ref[a + i] = diagonal
    for a in range(links):
        ident = adj_ref[s, a]
        rel = (ident // owner_links) ^ sub
        slot = count_ref[rel]
        count_ref[rel] = slot + 1
        at = rel * CAP + slot
        local_ref[at] = ident % blk_dev
        all_ref[at] = part_ref[a]
        side_ref[at] = edge_ref[a]

    @pl.when(s == pl.num_programs(0) - 1)
    def _():
        half = block // 2
        row = lax.broadcasted_iota(jnp.int32, (TAIL, block), 0)
        lane = lax.broadcasted_iota(jnp.int32, (TAIL, block), 1)
        for d, out in enumerate(outs):
            tail = jnp.zeros((TAIL, block), jnp.float32)
            for i in range(CAP):
                out[i * half:(i + 1) * half] = all_ref[d * CAP + i]
                place = local_ref[d * CAP + i].astype(jnp.float32)
                tail = jnp.where(
                    row == i, jnp.where(lane < half, side_ref[d * CAP + i], place), tail
                )
            out[CAP * half:] = tail.astype(jnp.bfloat16)


def make_contrib(modes, coupling, inv_eig, sub_rows, adjacency, n_sub, owner_links, blk_dev):
    subs, rows, width = modes.shape
    links, block = coupling.shape[1], coupling.shape[3]
    out = jax.ShapeDtypeStruct((CAP * block // 2 + TAIL, block), jnp.bfloat16)
    return pl.pallas_call(
        functools.partial(contrib_kernel, owner_links, blk_dev, n_sub),
        grid=(subs,),
        in_specs=[
            SMEM, SMEM,
            pl.BlockSpec((1, rows, width), lambda s: (s, 0, 0)),
            pl.BlockSpec((1, links, rows, block), lambda s: (s, 0, 0, 0)),
            pl.BlockSpec(inv_eig.shape, lambda s: (0, 0)),
        ],
        out_specs=[pl.BlockSpec(out.shape, lambda s: (0, 0))] * n_sub,
        out_shape=[out] * n_sub,
        scratch_shapes=[
            pltpu.VMEM((links, block // 2, block), jnp.bfloat16),
            pltpu.VMEM((links, 1, block), jnp.float32),
            pltpu.VMEM((n_sub * CAP, block // 2, block), jnp.bfloat16),
            pltpu.VMEM((n_sub * CAP, 1, block), jnp.float32),
            pltpu.SMEM((n_sub,), jnp.int32),
            pltpu.SMEM((n_sub * CAP,), jnp.int32),
        ],
        compiler_params=params(55),
        cost_estimate=cheap(),
        name="contrib",
    )(sub_rows, adjacency, modes, coupling, inv_eig)


def add_groups(upper_ref, side_ref, groups):
    half, block = upper_ref.shape[1:]
    for group in groups:
        tail = group[CAP * half:].astype(jnp.float32)
        for i in range(CAP):
            place = jnp.max(tail[i:i + 1, half:]).astype(jnp.int32)
            upper_ref[place] += group[i * half:(i + 1) * half].astype(jnp.float32)
            side_ref[place] += tail[i:i + 1]


def near_kernel(own_ref, pair_ref, upper_ref, side_ref):
    upper_ref[...] = jnp.zeros_like(upper_ref)
    side_ref[...] = jnp.zeros_like(side_ref)
    add_groups(upper_ref, side_ref, (own_ref, pair_ref))


def make_near(blk_dev, groups):
    block = groups[0].shape[1]
    shapes = [(blk_dev + 1, block // 2, block), (blk_dev + 1, 1, block)]
    return pl.pallas_call(
        near_kernel,
        in_specs=[VMEM] * 2,
        out_specs=[VMEM] * 2,
        out_shape=[jax.ShapeDtypeStruct(v, jnp.float32) for v in shapes],
        compiler_params=params(12),
        cost_estimate=cheap(),
        name="near",
    )(*groups)


def far_kernel(count, base_ref, near_ref, near_side_ref, *rest):
    mass_ref, upper_ref, side_ref = rest[-3:]
    upper_ref[...] = near_ref[...]
    side_ref[...] = near_side_ref[...]
    add_groups(upper_ref, side_ref, rest[:count])
    for b in range(mass_ref.shape[0]):
        mass_ref[b] = (base_ref[b] + unpack(upper_ref[b], side_ref[b])).astype(jnp.bfloat16)


def make_far(base, near, groups, behind):
    return pl.pallas_call(
        functools.partial(far_kernel, len(groups)),
        in_specs=[VMEM] * (3 + len(groups)) + [ANY] * len(behind),
        out_specs=VMEM,
        out_shape=jax.ShapeDtypeStruct(base.shape, jnp.bfloat16),
        scratch_shapes=[pltpu.VMEM(v.shape, jnp.float32) for v in near],
        compiler_params=params(12),
        cost_estimate=cheap(),
        name="far",
    )(base, *near, *groups, *behind)


def turn_kernel(psi_ref, out_ref, copy_ref, sems):
    band, n_sub = out_ref.shape[1], sems.shape[0]

    def bring(j):
        at = pl.ds(pl.multiple_of((lax.axis_index("sub") ^ j) * band, band), band)
        return pltpu.make_async_copy(psi_ref.at[:, at], copy_ref.at[:, at], sems.at[j])

    order = list(range(0, n_sub, CORES)) + [j for j in range(n_sub) if j % CORES]
    for j in order:
        bring(j).start()
    for j in order:
        bring(j).wait()
        if j % CORES == 0:
            at = pl.multiple_of((lax.axis_index("sub") ^ j) * band, band)
            out_ref[j // CORES] = copy_ref[:, pl.ds(at, band)].T


def turn(psi, n_sub):
    depth, width = psi.shape
    shape = (n_sub // CORES, width // n_sub, depth)
    return pl.pallas_call(
        turn_kernel,
        in_specs=[ANY],
        out_specs=[VMEM, VMEM],
        out_shape=[
            jax.ShapeDtypeStruct(shape, psi.dtype), jax.ShapeDtypeStruct(psi.shape, psi.dtype)
        ],
        scratch_shapes=[pltpu.SemaphoreType.DMA((n_sub,))],
        compiler_params=params(16),
        cost_estimate=cheap(),
        name="turn",
    )(psi)


def turn_own_kernel(psi_ref, out_ref):
    n_x, band = out_ref.shape[:2]
    for x in range(n_x):
        at = pl.multiple_of((lax.axis_index("sub") ^ (x * CORES)) * band, band)
        out_ref[x] = psi_ref[:, pl.ds(at, band)].T


def turn_own(psi, n_sub):
    depth, width = psi.shape
    return pl.pallas_call(
        turn_own_kernel,
        in_specs=[VMEM],
        out_specs=VMEM,
        out_shape=jax.ShapeDtypeStruct((n_sub // CORES, width // n_sub, depth), psi.dtype),
        compiler_params=params(16),
        cost_estimate=cheap(),
        name="turn_own",
    )(psi)


def left_kernel(mass_ref, turned_ref, out_ref):
    block = mass_ref.shape[1]
    zero = jnp.zeros((block, block), jnp.bfloat16)
    groups, half, _ = turned_ref.shape
    for j in range(0, mass_ref.shape[0], 2):
        pair = jnp.concatenate(
            [
                jnp.concatenate([mass_ref[j], zero], axis=1),
                jnp.concatenate([zero, mass_ref[j + 1]], axis=1),
            ],
            axis=0,
        )
        cols = slice(j * block, (j + 2) * block)
        out_ref[:, cols] = jnp.dot(
            turned_ref[:, :, cols].reshape(groups * half, 2 * block), pair,
            preferred_element_type=jnp.float32,
        ).astype(jnp.bfloat16)


def head_kernel(chunk, acc_in, mass_ref, turned_ref, psi_ref, *refs):
    left_ref = refs[-1]
    left_kernel(mass_ref, turned_ref, left_ref)
    product_kernel(chunk, 1, acc_in, True, False, 0, left_ref, psi_ref, *refs[:-1])


def make_head(chunk, mass, turned, psi, band, width, go, acc=()):
    n_x, _, depth = turned.shape
    flops = 4 * band * width * depth
    return pl.pallas_call(
        functools.partial(head_kernel, chunk, bool(acc)),
        in_specs=[VMEM] * (3 + len(acc)),
        out_specs=[VMEM] * 2,
        out_shape=[
            jax.ShapeDtypeStruct((2, band, width), go),
            jax.ShapeDtypeStruct((n_x * band, depth), jnp.bfloat16),
        ],
        compiler_params=params(16),
        cost_estimate=pl.CostEstimate(
            flops=flops, bytes_accessed=flops // 512, transcendentals=0
        ),
        name="head",
    )(mass, turned, psi, *acc)


def make_left(mass, turned):
    groups, half, depth = turned.shape
    return pl.pallas_call(
        left_kernel,
        in_specs=[VMEM, VMEM],
        out_specs=VMEM,
        out_shape=jax.ShapeDtypeStruct((groups * half, depth), jnp.bfloat16),
        compiler_params=params(16),
        cost_estimate=cheap(),
        name="left",
    )(mass, turned)


def product_kernel(chunk, pairs, acc_in, go, keep, behind, *refs):
    lefts, psis, refs = refs[:pairs], refs[pairs:2 * pairs], refs[2 * pairs:]
    acc = refs[0] if acc_in else None
    outs = list(refs[int(acc_in) + behind:])
    high, z = chunk
    core = lax.axis_index("sub") % CORES

    def block(x, y):
        band, width = outs[0].shape[1:]
        rows = pl.ds(pl.multiple_of((2 * high + x) * band, band), band)
        tile = lax.axis_index("tile") ^ (2 * z + y)
        cols = pl.ds(pl.multiple_of(tile * width, width), width)
        res = None
        for left, psi in zip(lefts, psis):
            term = jnp.dot(left[rows], psi[:, cols], preferred_element_type=jnp.float32)
            res = term if res is None else res + term
        return res

    places = []
    if go:
        places += [(outs[0], 0, 1, 1), (outs[0], 1, 1 - core, core)]
    if keep:
        places += [(outs[-1], 0, 0, 0), (outs[-1], 1, core, 1 - core)]
    for out, i, x, y in places:
        res = block(x, y)
        if acc_in:
            res += acc[i]
        out[i] = res.astype(out.dtype)


def product(chunk, lefts, psis, band, width, go=None, keep=False, acc=(), behind=()):
    depth = lefts[0].shape[1]
    types = ([go] if go is not None else []) + ([jnp.float32] if keep else [])
    flops = len(types) * 4 * band * width * depth * len(lefts)
    return pl.pallas_call(
        functools.partial(
            product_kernel, chunk, len(lefts), bool(acc), go is not None, keep, len(behind)
        ),
        in_specs=[VMEM] * (2 * len(lefts) + len(acc)) + [ANY] * len(behind),
        out_specs=[VMEM] * len(types),
        out_shape=[jax.ShapeDtypeStruct((2, band, width), t) for t in types],
        compiler_params=params(16),
        cost_estimate=pl.CostEstimate(
            flops=flops, bytes_accessed=flops // 512, transcendentals=0
        ),
        name="product",
    )(*lefts, *psis, *acc, *behind)


def first_kernel(keep_ref, got_ref, *refs):
    low_ref, go_ref = refs[-2:]
    low_ref[...] = keep_ref[0] + got_ref[1].astype(jnp.float32)
    go_ref[...] = (keep_ref[1] + got_ref[0].astype(jnp.float32)).astype(jnp.bfloat16)


def add_first(keep, got, behind=()):
    shape = keep.shape[1:]
    return pl.pallas_call(
        first_kernel,
        in_specs=[VMEM] * 2 + [ANY] * len(behind),
        out_specs=[VMEM] * 2,
        out_shape=[jax.ShapeDtypeStruct(shape, t) for t in (jnp.float32, jnp.bfloat16)],
        compiler_params=params(12),
        cost_estimate=cheap(),
        name="add_first",
    )(keep, got, *behind)


def second_kernel(low_ref, got_ref, *refs):
    total = low_ref[...] + got_ref[...].astype(jnp.float32)
    for v in refs[:-1]:
        total += v[...].astype(jnp.float32)
    refs[-1][...] = total.astype(refs[-1].dtype)


def add_second(low, got, dtype, tails=()):
    return pl.pallas_call(
        second_kernel,
        in_specs=[VMEM] * (2 + len(tails)),
        out_specs=VMEM,
        out_shape=jax.ShapeDtypeStruct(low.shape, dtype),
        compiler_params=params(12),
        cost_estimate=cheap(),
        name="add_second",
    )(low, got, *tails)


def on_device(modes, coupling, inv_eig, sub_rows, adjacency, base_mass, iface_modes):
    n_sub = lax.axis_size("sub")
    n_tile = lax.axis_size("tile")
    blk_dev = base_mass.shape[0]
    owner_links = blk_dev * n_tile
    width = iface_modes.shape[1]
    band, tile = width // n_sub, width // n_tile
    def swap_sub(v, d):
        return lax.ppermute(v, "sub", [(i, i ^ d) for i in range(n_sub)])

    def swap(v, partner):
        pairs = []
        for i in range(n_sub):
            for j in range(n_tile):
                k, m = partner(i, j)
                pairs.append((i * n_tile + j, k * n_tile + m))
        return lax.ppermute(v, ("sub", "tile"), pairs)

    def swap_first(v):
        return swap(v, lambda i, j: (i, j ^ 1) if i % CORES else (i ^ CORES, j))

    def swap_second(v):
        return swap(v, lambda i, j: (i ^ CORES, j) if i % CORES else (i, j ^ 1))

    def swap_third(v, chunk):
        high, z = chunk
        bit = z & -z if z else 0
        step = 0 if z else (high & -high) * 2 * CORES
        return swap(v, lambda i, j: (i ^ step, j ^ (2 * bit)))

    other = swap_sub(iface_modes, 1)
    sent = make_contrib(
        modes, coupling, inv_eig, sub_rows, adjacency, n_sub, owner_links, blk_dev
    )
    far = [swap_sub(sent[d], d) for d in range(CORES, n_sub)]
    near = make_near(blk_dev, [sent[0], swap_sub(sent[1], 1)])
    own_t, own = turn_own(iface_modes, n_sub), iface_modes
    other_t, other = turn(other, n_sub)
    mass = make_far(base_mass, near, far, [own_t, other_t])
    mass_other = swap_sub(mass, 1)

    chunks = [(h, z) for h in range(n_sub // (2 * CORES)) for z in range(n_tile // 2)][::-1]
    goes_to = {(h, z): (h, z & (z - 1)) if z else (h & (h - 1), 0) for h, z in chunks[:-1]}
    head, left = make_head(chunks[0], mass, own_t, own, band, tile, jnp.float32)
    go, left_other = make_head(
        chunks[0], mass_other, other_t, other, band, tile, jnp.bfloat16, [head]
    )
    lefts, psis = [left, left_other], [own, other]

    keep, first, second, third = {}, {}, {}, {}
    tails = {c: [] for c in chunks}
    last = len(chunks) - 1
    common = lefts, psis, band, tile
    for i in range(last + 1):
        first[i] = swap_first(go)
        if i < last:
            behind = [second[i - 1][0]] if i else [go]
            go, = product(chunks[i + 1], *common, go=jnp.bfloat16, behind=behind)
        behind = [go] + ([third[i - 2]] if i - 2 in third else [])
        keep[i], = product(chunks[i], *common, keep=True, behind=behind)
        behind = [third[i - 2]] if 0 and i > 1 else []
        low, move = add_first(keep[i], first[i], behind)
        second[i] = low, swap_second(move)
        if i:
            chunk = chunks[i - 1]
            third[i - 1] = add_second(*second[i - 1], jnp.bfloat16, tails[chunk])
            tails[goes_to[chunk]].append(swap_third(third[i - 1], chunk))
    low, got = second[last]
    early, late = [got] + tails[chunks[-1]][:-1], tails[chunks[-1]][-1:]
    if early:
        low = add_second(low, early[0], jnp.float32, early[1:])
    return add_second(low, late[0], jnp.float32, late[1:])


def solution(mesh):
    placed = (
        P(("sub", "tile"), None, None),
        P(("sub", "tile"), None, None, None),
        P(("sub", "tile"), None),
        P(("sub", "tile")),
        P(("sub", "tile"), None),
        P(("sub", "tile"), None, None),
        P(("sub", "tile"), None),
    )
    return jax.shard_map(
        on_device, mesh=mesh, in_specs=placed, out_specs=P("sub", "tile"), check_vma=False
    )
```

```python
import functools

import jax
import jax.numpy as jnp
from jax import lax
from jax.experimental import pallas as pl
from jax.experimental.pallas import tpu as pltpu
from jax.sharding import PartitionSpec as P

CAP = 8
TAIL = 16
CORES = 2
MIB = 1024 * 1024
SMEM = pl.BlockSpec(memory_space=pltpu.SMEM)
VMEM = pl.BlockSpec(memory_space=pltpu.VMEM)


def params(mib):
    return pltpu.CompilerParams(vmem_limit_bytes=mib * MIB)


def cheap():
    return pl.CostEstimate(flops=1, bytes_accessed=1, transcendentals=0)


ANY = pl.BlockSpec(memory_space=pl.ANY)


def corner(block):
    row = lax.broadcasted_iota(jnp.int32, (block // 2, block), 0)
    return row, lax.broadcasted_iota(jnp.int32, (block // 2, block), 1)


def pack(square):
    block = square.shape[0]
    half = block // 2
    row, lane = corner(block)
    last = pltpu.roll(square[half:], half, 1)
    upper = jnp.where(lane < row, last, square[:half])
    diagonal = jnp.sum(jnp.where(lane == row, last, 0.0), axis=0, keepdims=True)
    return upper.astype(jnp.bfloat16), diagonal


def unpack(upper, diagonal):
    block = upper.shape[1]
    half = block // 2
    row, lane = corner(block)
    top = jnp.where(lane > row, upper, jnp.where(lane == row, 0.5 * upper, 0.0))
    low = jnp.where(lane < row, upper, jnp.where(lane == row, 0.5 * diagonal, 0.0))
    square = jnp.concatenate([top, pltpu.roll(low, half, 1)], axis=0)
    return square + square.T


def contrib_kernel(
    owner_links, blk_dev, n_sub, rows_ref, adj_ref, modes_ref, coup_ref, inv_ref, *refs
):
    outs = refs[:n_sub]
    part_ref, edge_ref, all_ref, side_ref, count_ref, local_ref = refs[n_sub:]
    s = pl.program_id(0)
    sub = lax.axis_index("sub")
    links, rows, block = coup_ref.shape[1:]

    @pl.when(s == 0)
    def _():
        for d in range(n_sub):
            count_ref[d] = 0
            for i in range(CAP):
                local_ref[d * CAP + i] = blk_dev

    live = lax.broadcasted_iota(jnp.int32, (rows, 1), 0) < rows_ref[s]
    modes = jnp.where(live, modes_ref[0], jnp.zeros((), modes_ref.dtype))
    inv = inv_ref[pl.ds(s, 1), :]
    wide = jnp.concatenate([coup_ref[0, a] for a in range(links)], axis=1)
    red = lax.dot_general(
        wide, modes, (((0,), (0,)), ((), ())), preferred_element_type=jnp.float32
    )
    weighted = (red * inv).astype(jnp.bfloat16)
    red_b = red.astype(jnp.bfloat16)
    group = 2 if links % 2 == 0 else 1
    for a in range(0, links, group):
        part = slice(a * block, (a + group) * block)
        square = lax.dot_general(
            weighted[part], red_b[part], (((1,), (1,)), ((), ())),
            preferred_element_type=jnp.float32,
        )
        for i in range(group):
            here = slice(i * block, (i + 1) * block)
            upper, diagonal = pack(square[here, here])
            part_ref[a + i] = upper
            edge_ref[a + i] = diagonal
    for a in range(links):
        ident = adj_ref[s, a]
        rel = (ident // owner_links) ^ sub
        slot = count_ref[rel]
        count_ref[rel] = slot + 1
        at = rel * CAP + slot
        local_ref[at] = ident % blk_dev
        all_ref[at] = part_ref[a]
        side_ref[at] = edge_ref[a]

    @pl.when(s == pl.num_programs(0) - 1)
    def _():
        half = block // 2
        row = lax.broadcasted_iota(jnp.int32, (TAIL, block), 0)
        lane = lax.broadcasted_iota(jnp.int32, (TAIL, block), 1)
        for d, out in enumerate(outs):
            tail = jnp.zeros((TAIL, block), jnp.float32)
            for i in range(CAP):
                out[i * half:(i + 1) * half] = all_ref[d * CAP + i]
                place = local_ref[d * CAP + i].astype(jnp.float32)
                tail = jnp.where(
                    row == i, jnp.where(lane < half, side_ref[d * CAP + i], place), tail
                )
            out[CAP * half:] = tail.astype(jnp.bfloat16)


def make_contrib(modes, coupling, inv_eig, sub_rows, adjacency, n_sub, owner_links, blk_dev):
    subs, rows, width = modes.shape
    links, block = coupling.shape[1], coupling.shape[3]
    out = jax.ShapeDtypeStruct((CAP * block // 2 + TAIL, block), jnp.bfloat16)
    return pl.pallas_call(
        functools.partial(contrib_kernel, owner_links, blk_dev, n_sub),
        grid=(subs,),
        in_specs=[
            SMEM, SMEM,
            pl.BlockSpec((1, rows, width), lambda s: (s, 0, 0)),
            pl.BlockSpec((1, links, rows, block), lambda s: (s, 0, 0, 0)),
            pl.BlockSpec(inv_eig.shape, lambda s: (0, 0)),
        ],
        out_specs=[pl.BlockSpec(out.shape, lambda s: (0, 0))] * n_sub,
        out_shape=[out] * n_sub,
        scratch_shapes=[
            pltpu.VMEM((links, block // 2, block), jnp.bfloat16),
            pltpu.VMEM((links, 1, block), jnp.float32),
            pltpu.VMEM((n_sub * CAP, block // 2, block), jnp.bfloat16),
            pltpu.VMEM((n_sub * CAP, 1, block), jnp.float32),
            pltpu.SMEM((n_sub,), jnp.int32),
            pltpu.SMEM((n_sub * CAP,), jnp.int32),
        ],
        compiler_params=params(55),
        cost_estimate=cheap(),
        name="contrib",
    )(sub_rows, adjacency, modes, coupling, inv_eig)


def add_groups(upper_ref, side_ref, groups):
    half, block = upper_ref.shape[1:]
    for group in groups:
        tail = group[CAP * half:].astype(jnp.float32)
        for i in range(CAP):
            place = jnp.max(tail[i:i + 1, half:]).astype(jnp.int32)
            upper_ref[place] += group[i * half:(i + 1) * half].astype(jnp.float32)
            side_ref[place] += tail[i:i + 1]


def near_kernel(own_ref, pair_ref, upper_ref, side_ref):
    upper_ref[...] = jnp.zeros_like(upper_ref)
    side_ref[...] = jnp.zeros_like(side_ref)
    add_groups(upper_ref, side_ref, (own_ref, pair_ref))


def make_near(blk_dev, groups):
    block = groups[0].shape[1]
    shapes = [(blk_dev + 1, block // 2, block), (blk_dev + 1, 1, block)]
    return pl.pallas_call(
        near_kernel,
        in_specs=[VMEM] * 2,
        out_specs=[VMEM] * 2,
        out_shape=[jax.ShapeDtypeStruct(v, jnp.float32) for v in shapes],
        compiler_params=params(12),
        cost_estimate=cheap(),
        name="near",
    )(*groups)


def far_kernel(count, base_ref, near_ref, near_side_ref, *rest):
    mass_ref, upper_ref, side_ref = rest[-3:]
    upper_ref[...] = near_ref[...]
    side_ref[...] = near_side_ref[...]
    add_groups(upper_ref, side_ref, rest[:count])
    for b in range(mass_ref.shape[0]):
        mass_ref[b] = (base_ref[b] + unpack(upper_ref[b], side_ref[b])).astype(jnp.bfloat16)


def make_far(base, near, groups, behind):
    return pl.pallas_call(
        functools.partial(far_kernel, len(groups)),
        in_specs=[VMEM] * (3 + len(groups)) + [ANY] * len(behind),
        out_specs=VMEM,
        out_shape=jax.ShapeDtypeStruct(base.shape, jnp.bfloat16),
        scratch_shapes=[pltpu.VMEM(v.shape, jnp.float32) for v in near],
        compiler_params=params(12),
        cost_estimate=cheap(),
        name="far",
    )(base, *near, *groups, *behind)


def turn_kernel(psi_ref, out_ref, copy_ref, sems):
    band, n_sub = out_ref.shape[1], sems.shape[0]

    def bring(j):
        at = pl.ds(pl.multiple_of((lax.axis_index("sub") ^ j) * band, band), band)
        return pltpu.make_async_copy(psi_ref.at[:, at], copy_ref.at[:, at], sems.at[j])

    order = list(range(0, n_sub, CORES)) + [j for j in range(n_sub) if j % CORES]
    for j in order:
        bring(j).start()
    for j in order:
        bring(j).wait()
        if j % CORES == 0:
            at = pl.multiple_of((lax.axis_index("sub") ^ j) * band, band)
            out_ref[j // CORES] = copy_ref[:, pl.ds(at, band)].T


def turn(psi, n_sub):
    depth, width = psi.shape
    shape = (n_sub // CORES, width // n_sub, depth)
    return pl.pallas_call(
        turn_kernel,
        in_specs=[ANY],
        out_specs=[VMEM, VMEM],
        out_shape=[
            jax.ShapeDtypeStruct(shape, psi.dtype), jax.ShapeDtypeStruct(psi.shape, psi.dtype)
        ],
        scratch_shapes=[pltpu.SemaphoreType.DMA((n_sub,))],
        compiler_params=params(16),
        cost_estimate=cheap(),
        name="turn",
    )(psi)


def turn_own_kernel(psi_ref, out_ref):
    n_x, band = out_ref.shape[:2]
    for x in range(n_x):
        at = pl.multiple_of((lax.axis_index("sub") ^ (x * CORES)) * band, band)
        out_ref[x] = psi_ref[:, pl.ds(at, band)].T


def turn_own(psi, n_sub):
    depth, width = psi.shape
    return pl.pallas_call(
        turn_own_kernel,
        in_specs=[VMEM],
        out_specs=VMEM,
        out_shape=jax.ShapeDtypeStruct((n_sub // CORES, width // n_sub, depth), psi.dtype),
        compiler_params=params(16),
        cost_estimate=cheap(),
        name="turn_own",
    )(psi)


def left_kernel(mass_ref, turned_ref, out_ref):
    block = mass_ref.shape[1]
    zero = jnp.zeros((block, block), jnp.bfloat16)
    groups, half, _ = turned_ref.shape
    for j in range(0, mass_ref.shape[0], 2):
        pair = jnp.concatenate(
            [
                jnp.concatenate([mass_ref[j], zero], axis=1),
                jnp.concatenate([zero, mass_ref[j + 1]], axis=1),
            ],
            axis=0,
        )
        cols = slice(j * block, (j + 2) * block)
        out_ref[:, cols] = jnp.dot(
            turned_ref[:, :, cols].reshape(groups * half, 2 * block), pair,
            preferred_element_type=jnp.float32,
        ).astype(jnp.bfloat16)


def head_kernel(chunk, acc_in, mass_ref, turned_ref, psi_ref, *refs):
    left_ref = refs[-1]
    left_kernel(mass_ref, turned_ref, left_ref)
    product_kernel(chunk, 1, acc_in, True, False, 0, left_ref, psi_ref, *refs[:-1])


def make_head(chunk, mass, turned, psi, band, width, go, acc=()):
    n_x, _, depth = turned.shape
    flops = 4 * band * width * depth
    return pl.pallas_call(
        functools.partial(head_kernel, chunk, bool(acc)),
        in_specs=[VMEM] * (3 + len(acc)),
        out_specs=[VMEM] * 2,
        out_shape=[
            jax.ShapeDtypeStruct((2, band, width), go),
            jax.ShapeDtypeStruct((n_x * band, depth), jnp.bfloat16),
        ],
        compiler_params=params(16),
        cost_estimate=pl.CostEstimate(
            flops=flops, bytes_accessed=flops // 512, transcendentals=0
        ),
        name="head",
    )(mass, turned, psi, *acc)


def make_left(mass, turned):
    groups, half, depth = turned.shape
    return pl.pallas_call(
        left_kernel,
        in_specs=[VMEM, VMEM],
        out_specs=VMEM,
        out_shape=jax.ShapeDtypeStruct((groups * half, depth), jnp.bfloat16),
        compiler_params=params(16),
        cost_estimate=cheap(),
        name="left",
    )(mass, turned)


def product_kernel(chunk, pairs, acc_in, go, keep, behind, *refs):
    lefts, psis, refs = refs[:pairs], refs[pairs:2 * pairs], refs[2 * pairs:]
    acc = refs[0] if acc_in else None
    outs = list(refs[int(acc_in) + behind:])
    high, z = chunk
    core = lax.axis_index("sub") % CORES

    def block(x, y):
        band, width = outs[0].shape[1:]
        rows = pl.ds(pl.multiple_of((2 * high + x) * band, band), band)
        tile = lax.axis_index("tile") ^ (2 * z + y)
        cols = pl.ds(pl.multiple_of(tile * width, width), width)
        res = None
        for left, psi in zip(lefts, psis):
            term = jnp.dot(left[rows], psi[:, cols], preferred_element_type=jnp.float32)
            res = term if res is None else res + term
        return res

    places = []
    if go:
        places += [(outs[0], 0, 1, 1), (outs[0], 1, 1 - core, core)]
    if keep:
        places += [(outs[-1], 0, 0, 0), (outs[-1], 1, core, 1 - core)]
    for out, i, x, y in places:
        res = block(x, y)
        if acc_in:
            res += acc[i]
        out[i] = res.astype(out.dtype)


def product(chunk, lefts, psis, band, width, go=None, keep=False, acc=(), behind=()):
    depth = lefts[0].shape[1]
    types = ([go] if go is not None else []) + ([jnp.float32] if keep else [])
    flops = len(types) * 4 * band * width * depth * len(lefts)
    return pl.pallas_call(
        functools.partial(
            product_kernel, chunk, len(lefts), bool(acc), go is not None, keep, len(behind)
        ),
        in_specs=[VMEM] * (2 * len(lefts) + len(acc)) + [ANY] * len(behind),
        out_specs=[VMEM] * len(types),
        out_shape=[jax.ShapeDtypeStruct((2, band, width), t) for t in types],
        compiler_params=params(16),
        cost_estimate=pl.CostEstimate(
            flops=flops, bytes_accessed=flops // 512, transcendentals=0
        ),
        name="product",
    )(*lefts, *psis, *acc, *behind)


def first_kernel(keep_ref, got_ref, *refs):
    low_ref, go_ref = refs[-2:]
    low_ref[...] = keep_ref[0] + got_ref[1].astype(jnp.float32)
    go_ref[...] = (keep_ref[1] + got_ref[0].astype(jnp.float32)).astype(jnp.bfloat16)


def add_first(keep, got, behind=()):
    shape = keep.shape[1:]
    return pl.pallas_call(
        first_kernel,
        in_specs=[VMEM] * 2 + [ANY] * len(behind),
        out_specs=[VMEM] * 2,
        out_shape=[jax.ShapeDtypeStruct(shape, t) for t in (jnp.float32, jnp.bfloat16)],
        compiler_params=params(12),
        cost_estimate=cheap(),
        name="add_first",
    )(keep, got, *behind)


def second_kernel(low_ref, got_ref, *refs):
    total = low_ref[...] + got_ref[...].astype(jnp.float32)
    for v in refs[:-1]:
        total += v[...].astype(jnp.float32)
    refs[-1][...] = total.astype(refs[-1].dtype)


def add_second(low, got, dtype, tails=()):
    return pl.pallas_call(
        second_kernel,
        in_specs=[VMEM] * (2 + len(tails)),
        out_specs=VMEM,
        out_shape=jax.ShapeDtypeStruct(low.shape, dtype),
        compiler_params=params(12),
        cost_estimate=cheap(),
        name="add_second",
    )(low, got, *tails)


def last_kernel(low_ref, *refs):
    tails, (out_ref, held_ref, sems) = refs[:-3], refs[-3:]
    pieces = sems.shape[0]
    rows = low_ref.shape[0] // pieces
    copies = []
    for i in range(pieces):
        here = pl.ds(i * rows, rows)
        total = low_ref[here]
        for v in tails:
            total += v[here].astype(jnp.float32)
        held_ref[here] = total
        copies.append(pltpu.make_async_copy(held_ref.at[here], out_ref.at[here], sems.at[i]))
        copies[-1].start()
    for copy in copies:
        copy.wait()


def add_last(low, tails):
    return pl.pallas_call(
        last_kernel,
        in_specs=[VMEM] * (1 + len(tails)),
        out_specs=ANY,
        out_shape=jax.ShapeDtypeStruct(low.shape, jnp.float32),
        scratch_shapes=[pltpu.VMEM(low.shape, jnp.float32), pltpu.SemaphoreType.DMA((4,))],
        compiler_params=params(12),
        cost_estimate=cheap(),
        name="add_last",
    )(low, *tails)


def on_device(modes, coupling, inv_eig, sub_rows, adjacency, base_mass, iface_modes):
    n_sub = lax.axis_size("sub")
    n_tile = lax.axis_size("tile")
    blk_dev = base_mass.shape[0]
    owner_links = blk_dev * n_tile
    width = iface_modes.shape[1]
    band, tile = width // n_sub, width // n_tile
    def swap_sub(v, d):
        return lax.ppermute(v, "sub", [(i, i ^ d) for i in range(n_sub)])

    def swap(v, partner):
        pairs = []
        for i in range(n_sub):
            for j in range(n_tile):
                k, m = partner(i, j)
                pairs.append((i * n_tile + j, k * n_tile + m))
        return lax.ppermute(v, ("sub", "tile"), pairs)

    def swap_first(v):
        return swap(v, lambda i, j: (i, j ^ 1) if i % CORES else (i ^ CORES, j))

    def swap_second(v):
        return swap(v, lambda i, j: (i ^ CORES, j) if i % CORES else (i, j ^ 1))

    def swap_third(v, chunk):
        high, z = chunk
        bit = z & -z if z else 0
        step = 0 if z else (high & -high) * 2 * CORES
        return swap(v, lambda i, j: (i ^ step, j ^ (2 * bit)))

    other = swap_sub(iface_modes, 1)
    sent = make_contrib(
        modes, coupling, inv_eig, sub_rows, adjacency, n_sub, owner_links, blk_dev
    )
    far = [swap_sub(sent[d], d) for d in range(CORES, n_sub)]
    near = make_near(blk_dev, [sent[0], swap_sub(sent[1], 1)])
    own_t, own = turn_own(iface_modes, n_sub), iface_modes
    other_t, other = turn(other, n_sub)
    mass = make_far(base_mass, near, far, [own_t, other_t])
    mass_other = swap_sub(mass, 1)

    chunks = [(h, z) for h in range(n_sub // (2 * CORES)) for z in range(n_tile // 2)][::-1]
    goes_to = {(h, z): (h, z & (z - 1)) if z else (h & (h - 1), 0) for h, z in chunks[:-1]}
    head, left = make_head(chunks[0], mass, own_t, own, band, tile, jnp.float32)
    go, left_other = make_head(
        chunks[0], mass_other, other_t, other, band, tile, jnp.bfloat16, [head]
    )
    lefts, psis = [left, left_other], [own, other]

    keep, first, second, third = {}, {}, {}, {}
    tails = {c: [] for c in chunks}
    last = len(chunks) - 1
    common = lefts, psis, band, tile
    for i in range(last + 1):
        first[i] = swap_first(go)
        if i < last:
            behind = [second[i - 1][0]] if i else [go]
            go, = product(chunks[i + 1], *common, go=jnp.bfloat16, behind=behind)
        behind = [go] + ([third[i - 2]] if i - 2 in third else [])
        keep[i], = product(chunks[i], *common, keep=True, behind=behind)
        behind = [third[i - 2]] if 0 and i > 1 else []
        low, move = add_first(keep[i], first[i], behind)
        second[i] = low, swap_second(move)
        if i:
            chunk = chunks[i - 1]
            third[i - 1] = add_second(*second[i - 1], jnp.bfloat16, tails[chunk])
            tails[goes_to[chunk]].append(swap_third(third[i - 1], chunk))
    low, got = second[last]
    early, late = [got] + tails[chunks[-1]][:-1], tails[chunks[-1]][-1:]
    if early:
        low = add_second(low, early[0], jnp.float32, early[1:])
    return add_last(low, late)


def solution(mesh):
    placed = (
        P(("sub", "tile"), None, None),
        P(("sub", "tile"), None, None, None),
        P(("sub", "tile"), None),
        P(("sub", "tile")),
        P(("sub", "tile"), None),
        P(("sub", "tile"), None, None),
        P(("sub", "tile"), None),
    )
    return jax.shard_map(
        on_device, mesh=mesh, in_specs=placed, out_specs=P("sub", "tile"), check_vma=False
    )
```

```python
import functools

import jax
import jax.numpy as jnp
from jax import lax
from jax.experimental import pallas as pl
from jax.experimental.pallas import tpu as pltpu
from jax.sharding import PartitionSpec as P

CAP = 8
TAIL = 16
CORES = 2
MIB = 1024 * 1024
SMEM = pl.BlockSpec(memory_space=pltpu.SMEM)
VMEM = pl.BlockSpec(memory_space=pltpu.VMEM)


def params(mib):
    return pltpu.CompilerParams(vmem_limit_bytes=mib * MIB)


def cheap():
    return pl.CostEstimate(flops=1, bytes_accessed=1, transcendentals=0)


ANY = pl.BlockSpec(memory_space=pl.ANY)


def corner(block):
    row = lax.broadcasted_iota(jnp.int32, (block // 2, block), 0)
    return row, lax.broadcasted_iota(jnp.int32, (block // 2, block), 1)


def pack(square):
    block = square.shape[0]
    half = block // 2
    row, lane = corner(block)
    last = pltpu.roll(square[half:], half, 1)
    upper = jnp.where(lane < row, last, square[:half])
    diagonal = jnp.sum(jnp.where(lane == row, last, 0.0), axis=0, keepdims=True)
    return upper.astype(jnp.bfloat16), diagonal


def unpack(upper, diagonal):
    block = upper.shape[1]
    half = block // 2
    row, lane = corner(block)
    top = jnp.where(lane > row, upper, jnp.where(lane == row, 0.5 * upper, 0.0))
    low = jnp.where(lane < row, upper, jnp.where(lane == row, 0.5 * diagonal, 0.0))
    square = jnp.concatenate([top, pltpu.roll(low, half, 1)], axis=0)
    return square + square.T


def contrib_kernel(
    owner_links, blk_dev, n_sub, rows_ref, adj_ref, modes_ref, coup_ref, inv_ref, *refs
):
    outs = refs[:n_sub]
    part_ref, edge_ref, all_ref, side_ref, count_ref, local_ref = refs[n_sub:]
    s = pl.program_id(0)
    sub = lax.axis_index("sub")
    links, rows, block = coup_ref.shape[1:]

    @pl.when(s == 0)
    def _():
        for d in range(n_sub):
            count_ref[d] = 0
            for i in range(CAP):
                local_ref[d * CAP + i] = blk_dev

    live = lax.broadcasted_iota(jnp.int32, (rows, 1), 0) < rows_ref[s]
    modes = jnp.where(live, modes_ref[0], jnp.zeros((), modes_ref.dtype))
    inv = inv_ref[pl.ds(s, 1), :]
    wide = jnp.concatenate([coup_ref[0, a] for a in range(links)], axis=1)
    red = lax.dot_general(
        wide, modes, (((0,), (0,)), ((), ())), preferred_element_type=jnp.float32
    )
    weighted = (red * inv).astype(jnp.bfloat16)
    red_b = red.astype(jnp.bfloat16)
    group = 2 if links % 2 == 0 else 1
    for a in range(0, links, group):
        part = slice(a * block, (a + group) * block)
        square = lax.dot_general(
            weighted[part], red_b[part], (((1,), (1,)), ((), ())),
            preferred_element_type=jnp.float32,
        )
        for i in range(group):
            here = slice(i * block, (i + 1) * block)
            upper, diagonal = pack(square[here, here])
            part_ref[a + i] = upper
            edge_ref[a + i] = diagonal
    for a in range(links):
        ident = adj_ref[s, a]
        rel = (ident // owner_links) ^ sub
        slot = count_ref[rel]
        count_ref[rel] = slot + 1
        at = rel * CAP + slot
        local_ref[at] = ident % blk_dev
        all_ref[at] = part_ref[a]
        side_ref[at] = edge_ref[a]

    @pl.when(s == pl.num_programs(0) - 1)
    def _():
        half = block // 2
        row = lax.broadcasted_iota(jnp.int32, (TAIL, block), 0)
        lane = lax.broadcasted_iota(jnp.int32, (TAIL, block), 1)
        for d, out in enumerate(outs):
            tail = jnp.zeros((TAIL, block), jnp.float32)
            for i in range(CAP):
                out[i * half:(i + 1) * half] = all_ref[d * CAP + i]
                place = local_ref[d * CAP + i].astype(jnp.float32)
                tail = jnp.where(
                    row == i, jnp.where(lane < half, side_ref[d * CAP + i], place), tail
                )
            out[CAP * half:] = tail.astype(jnp.bfloat16)


def make_contrib(modes, coupling, inv_eig, sub_rows, adjacency, n_sub, owner_links, blk_dev):
    subs, rows, width = modes.shape
    links, block = coupling.shape[1], coupling.shape[3]
    out = jax.ShapeDtypeStruct((CAP * block // 2 + TAIL, block), jnp.bfloat16)
    return pl.pallas_call(
        functools.partial(contrib_kernel, owner_links, blk_dev, n_sub),
        grid=(subs,),
        in_specs=[
            SMEM, SMEM,
            pl.BlockSpec((1, rows, width), lambda s: (s, 0, 0)),
            pl.BlockSpec((1, links, rows, block), lambda s: (s, 0, 0, 0)),
            pl.BlockSpec(inv_eig.shape, lambda s: (0, 0)),
        ],
        out_specs=[pl.BlockSpec(out.shape, lambda s: (0, 0))] * n_sub,
        out_shape=[out] * n_sub,
        scratch_shapes=[
            pltpu.VMEM((links, block // 2, block), jnp.bfloat16),
            pltpu.VMEM((links, 1, block), jnp.float32),
            pltpu.VMEM((n_sub * CAP, block // 2, block), jnp.bfloat16),
            pltpu.VMEM((n_sub * CAP, 1, block), jnp.float32),
            pltpu.SMEM((n_sub,), jnp.int32),
            pltpu.SMEM((n_sub * CAP,), jnp.int32),
        ],
        compiler_params=params(55),
        cost_estimate=cheap(),
        name="contrib",
    )(sub_rows, adjacency, modes, coupling, inv_eig)


def add_groups(upper_ref, side_ref, groups):
    half, block = upper_ref.shape[1:]
    for group in groups:
        tail = group[CAP * half:].astype(jnp.float32)
        for i in range(CAP):
            place = jnp.max(tail[i:i + 1, half:]).astype(jnp.int32)
            upper_ref[place] += group[i * half:(i + 1) * half].astype(jnp.float32)
            side_ref[place] += tail[i:i + 1]


def near_kernel(own_ref, pair_ref, upper_ref, side_ref):
    upper_ref[...] = jnp.zeros_like(upper_ref)
    side_ref[...] = jnp.zeros_like(side_ref)
    add_groups(upper_ref, side_ref, (own_ref, pair_ref))


def make_near(blk_dev, groups):
    block = groups[0].shape[1]
    shapes = [(blk_dev + 1, block // 2, block), (blk_dev + 1, 1, block)]
    return pl.pallas_call(
        near_kernel,
        in_specs=[VMEM] * 2,
        out_specs=[VMEM] * 2,
        out_shape=[jax.ShapeDtypeStruct(v, jnp.float32) for v in shapes],
        compiler_params=params(12),
        cost_estimate=cheap(),
        name="near",
    )(*groups)


def far_kernel(count, base_ref, near_ref, near_side_ref, *rest):
    mass_ref, upper_ref, side_ref = rest[-3:]
    upper_ref[...] = near_ref[...]
    side_ref[...] = near_side_ref[...]
    add_groups(upper_ref, side_ref, rest[:count])
    for b in range(mass_ref.shape[0]):
        mass_ref[b] = (base_ref[b] + unpack(upper_ref[b], side_ref[b])).astype(jnp.bfloat16)


def make_far(base, near, groups, behind):
    return pl.pallas_call(
        functools.partial(far_kernel, len(groups)),
        in_specs=[VMEM] * (3 + len(groups)) + [ANY] * len(behind),
        out_specs=VMEM,
        out_shape=jax.ShapeDtypeStruct(base.shape, jnp.bfloat16),
        scratch_shapes=[pltpu.VMEM(v.shape, jnp.float32) for v in near],
        compiler_params=params(12),
        cost_estimate=cheap(),
        name="far",
    )(base, *near, *groups, *behind)


def turn_kernel(psi_ref, out_ref, copy_ref, sems):
    band, n_sub = out_ref.shape[1], sems.shape[0]

    def bring(j):
        at = pl.ds(pl.multiple_of((lax.axis_index("sub") ^ j) * band, band), band)
        return pltpu.make_async_copy(psi_ref.at[:, at], copy_ref.at[:, at], sems.at[j])

    order = list(range(0, n_sub, CORES)) + [j for j in range(n_sub) if j % CORES]
    for j in order:
        bring(j).start()
    for j in order:
        bring(j).wait()
        if j % CORES == 0:
            at = pl.multiple_of((lax.axis_index("sub") ^ j) * band, band)
            out_ref[j // CORES] = copy_ref[:, pl.ds(at, band)].T


def turn(psi, n_sub):
    depth, width = psi.shape
    shape = (n_sub // CORES, width // n_sub, depth)
    return pl.pallas_call(
        turn_kernel,
        in_specs=[ANY],
        out_specs=[VMEM, VMEM],
        out_shape=[
            jax.ShapeDtypeStruct(shape, psi.dtype), jax.ShapeDtypeStruct(psi.shape, psi.dtype)
        ],
        scratch_shapes=[pltpu.SemaphoreType.DMA((n_sub,))],
        compiler_params=params(16),
        cost_estimate=cheap(),
        name="turn",
    )(psi)


def turn_own_kernel(psi_ref, out_ref):
    n_x, band = out_ref.shape[:2]
    for x in range(n_x):
        at = pl.multiple_of((lax.axis_index("sub") ^ (x * CORES)) * band, band)
        out_ref[x] = psi_ref[:, pl.ds(at, band)].T


def turn_own(psi, n_sub):
    depth, width = psi.shape
    return pl.pallas_call(
        turn_own_kernel,
        in_specs=[VMEM],
        out_specs=VMEM,
        out_shape=jax.ShapeDtypeStruct((n_sub // CORES, width // n_sub, depth), psi.dtype),
        compiler_params=params(16),
        cost_estimate=cheap(),
        name="turn_own",
    )(psi)


def left_kernel(mass_ref, turned_ref, out_ref):
    block = mass_ref.shape[1]
    zero = jnp.zeros((block, block), jnp.bfloat16)
    groups, half, _ = turned_ref.shape
    for j in range(0, mass_ref.shape[0], 2):
        pair = jnp.concatenate(
            [
                jnp.concatenate([mass_ref[j], zero], axis=1),
                jnp.concatenate([zero, mass_ref[j + 1]], axis=1),
            ],
            axis=0,
        )
        cols = slice(j * block, (j + 2) * block)
        out_ref[:, cols] = jnp.dot(
            turned_ref[:, :, cols].reshape(groups * half, 2 * block), pair,
            preferred_element_type=jnp.float32,
        ).astype(jnp.bfloat16)


def head_kernel(chunk, acc_in, mass_ref, turned_ref, psi_ref, *refs):
    left_ref = refs[-1]
    left_kernel(mass_ref, turned_ref, left_ref)
    product_kernel(chunk, 1, acc_in, True, False, 0, left_ref, psi_ref, *refs[:-1])


def make_head(chunk, mass, turned, psi, band, width, go, acc=()):
    n_x, _, depth = turned.shape
    flops = 4 * band * width * depth
    return pl.pallas_call(
        functools.partial(head_kernel, chunk, bool(acc)),
        in_specs=[VMEM] * (3 + len(acc)),
        out_specs=[VMEM] * 2,
        out_shape=[
            jax.ShapeDtypeStruct((2, band, width), go),
            jax.ShapeDtypeStruct((n_x * band, depth), jnp.bfloat16),
        ],
        compiler_params=params(16),
        cost_estimate=pl.CostEstimate(
            flops=flops, bytes_accessed=flops // 512, transcendentals=0
        ),
        name="head",
    )(mass, turned, psi, *acc)


def make_left(mass, turned):
    groups, half, depth = turned.shape
    return pl.pallas_call(
        left_kernel,
        in_specs=[VMEM, VMEM],
        out_specs=VMEM,
        out_shape=jax.ShapeDtypeStruct((groups * half, depth), jnp.bfloat16),
        compiler_params=params(16),
        cost_estimate=cheap(),
        name="left",
    )(mass, turned)


def product_kernel(chunk, pairs, acc_in, go, keep, behind, *refs):
    lefts, psis, refs = refs[:pairs], refs[pairs:2 * pairs], refs[2 * pairs:]
    acc = refs[0] if acc_in else None
    outs = list(refs[int(acc_in) + behind:])
    high, z = chunk
    core = lax.axis_index("sub") % CORES

    def block(x, y):
        band, width = outs[0].shape[1:]
        rows = pl.ds(pl.multiple_of((2 * high + x) * band, band), band)
        tile = lax.axis_index("tile") ^ (2 * z + y)
        cols = pl.ds(pl.multiple_of(tile * width, width), width)
        res = None
        for left, psi in zip(lefts, psis):
            term = jnp.dot(left[rows], psi[:, cols], preferred_element_type=jnp.float32)
            res = term if res is None else res + term
        return res

    places = []
    if go:
        places += [(outs[0], 0, 1, 1), (outs[0], 1, 1 - core, core)]
    if keep:
        places += [(outs[-1], 0, 0, 0), (outs[-1], 1, core, 1 - core)]
    for out, i, x, y in places:
        res = block(x, y)
        if acc_in:
            res += acc[i]
        out[i] = res.astype(out.dtype)


def product(chunk, lefts, psis, band, width, go=None, keep=False, acc=(), behind=()):
    depth = lefts[0].shape[1]
    types = ([go] if go is not None else []) + ([jnp.float32] if keep else [])
    flops = len(types) * 4 * band * width * depth * len(lefts)
    return pl.pallas_call(
        functools.partial(
            product_kernel, chunk, len(lefts), bool(acc), go is not None, keep, len(behind)
        ),
        in_specs=[VMEM] * (2 * len(lefts) + len(acc)) + [ANY] * len(behind),
        out_specs=[VMEM] * len(types),
        out_shape=[jax.ShapeDtypeStruct((2, band, width), t) for t in types],
        compiler_params=params(16),
        cost_estimate=pl.CostEstimate(
            flops=flops, bytes_accessed=flops // 512, transcendentals=0
        ),
        name="product",
    )(*lefts, *psis, *acc, *behind)


def first_kernel(keep_ref, got_ref, *refs):
    low_ref, go_ref = refs[-2:]
    low_ref[...] = keep_ref[0] + got_ref[1].astype(jnp.float32)
    go_ref[...] = (keep_ref[1] + got_ref[0].astype(jnp.float32)).astype(jnp.bfloat16)


def add_first(keep, got, behind=()):
    shape = keep.shape[1:]
    return pl.pallas_call(
        first_kernel,
        in_specs=[VMEM] * 2 + [ANY] * len(behind),
        out_specs=[VMEM] * 2,
        out_shape=[jax.ShapeDtypeStruct(shape, t) for t in (jnp.float32, jnp.bfloat16)],
        compiler_params=params(12),
        cost_estimate=cheap(),
        name="add_first",
    )(keep, got, *behind)


def second_kernel(low_ref, got_ref, *refs):
    total = low_ref[...] + got_ref[...].astype(jnp.float32)
    for v in refs[:-1]:
        total += v[...].astype(jnp.float32)
    refs[-1][...] = total.astype(refs[-1].dtype)


def add_second(low, got, dtype, tails=()):
    return pl.pallas_call(
        second_kernel,
        in_specs=[VMEM] * (2 + len(tails)),
        out_specs=VMEM,
        out_shape=jax.ShapeDtypeStruct(low.shape, dtype),
        compiler_params=params(12),
        cost_estimate=cheap(),
        name="add_second",
    )(low, got, *tails)


def on_device(modes, coupling, inv_eig, sub_rows, adjacency, base_mass, iface_modes):
    n_sub = lax.axis_size("sub")
    n_tile = lax.axis_size("tile")
    blk_dev = base_mass.shape[0]
    owner_links = blk_dev * n_tile
    width = iface_modes.shape[1]
    band, tile = width // n_sub, width // n_tile
    def swap_sub(v, d):
        return lax.ppermute(v, "sub", [(i, i ^ d) for i in range(n_sub)])

    def swap(v, partner):
        pairs = []
        for i in range(n_sub):
            for j in range(n_tile):
                k, m = partner(i, j)
                pairs.append((i * n_tile + j, k * n_tile + m))
        return lax.ppermute(v, ("sub", "tile"), pairs)

    def swap_first(v):
        return swap(v, lambda i, j: (i, j ^ 1) if i % CORES else (i ^ CORES, j))

    def swap_second(v):
        return swap(v, lambda i, j: (i ^ CORES, j) if i % CORES else (i, j ^ 1))

    def swap_third(v, chunk):
        high, z = chunk
        bit = z & -z if z else 0
        step = 0 if z else (high & -high) * 2 * CORES
        return swap(v, lambda i, j: (i ^ step, j ^ (2 * bit)))

    other = swap_sub(iface_modes, 1)
    sent = make_contrib(
        modes, coupling, inv_eig, sub_rows, adjacency, n_sub, owner_links, blk_dev
    )
    far = [swap_sub(sent[d], d) for d in range(CORES, n_sub)]
    near = make_near(blk_dev, [sent[0], swap_sub(sent[1], 1)])
    own_t, own = turn_own(iface_modes, n_sub), iface_modes
    other_t, other = turn(other, n_sub)
    mass = make_far(base_mass, near, far, [own_t, other_t])
    mass_other = swap_sub(mass, 1)

    chunks = [(h, z) for h in range(n_sub // (2 * CORES)) for z in range(n_tile // 2)][::-1]
    goes_to = {(h, z): (h, z & (z - 1)) if z else (h & (h - 1), 0) for h, z in chunks[:-1]}
    head, left = make_head(chunks[0], mass, own_t, own, band, tile, jnp.float32)
    go, left_other = make_head(
        chunks[0], mass_other, other_t, other, band, tile, jnp.bfloat16, [head]
    )
    lefts, psis = [left, left_other], [own, other]

    keep, first, second, third = {}, {}, {}, {}
    tails = {c: [] for c in chunks}
    last = len(chunks) - 1
    common = lefts, psis, band, tile
    for i in range(last + 1):
        first[i] = swap_first(go)
        if i < last:
            behind = [second[i - 1][0]] if i else [go]
            go, = product(chunks[i + 1], *common, go=jnp.bfloat16, behind=behind)
        behind = [keep[0]] if i == 1 else [go] + ([third[i - 2]] if i - 2 in third else [])
        keep[i], = product(chunks[i], *common, keep=True, behind=behind)
        behind = [third[i - 2]] if 0 and i > 1 else []
        low, move = add_first(keep[i], first[i], behind)
        second[i] = low, swap_second(move)
        if i:
            chunk = chunks[i - 1]
            third[i - 1] = add_second(*second[i - 1], jnp.bfloat16, tails[chunk])
            tails[goes_to[chunk]].append(swap_third(third[i - 1], chunk))
    low, got = second[last]
    early, late = [got] + tails[chunks[-1]][:-1], tails[chunks[-1]][-1:]
    if early:
        low = add_second(low, early[0], jnp.float32, early[1:])
    return add_second(low, late[0], jnp.float32, late[1:])


def solution(mesh):
    placed = (
        P(("sub", "tile"), None, None),
        P(("sub", "tile"), None, None, None),
        P(("sub", "tile"), None),
        P(("sub", "tile")),
        P(("sub", "tile"), None),
        P(("sub", "tile"), None, None),
        P(("sub", "tile"), None),
    )
    return jax.shard_map(
        on_device, mesh=mesh, in_specs=placed, out_specs=P("sub", "tile"), check_vma=False
    )
```
